32 devices in a mesh: dp: 16 (over z, y, x), tensor: 2 (over core).
Axes of the slice: x: 2, y: 2, z: 4, core: 2. Of those that a mesh axis runs over, the one named last changes fastest.
Arguments:
- tokens: bfloat16 [8192, 1024], P(('dp', 'tensor')), may hold values from -6 to 6
- block_kind: int32 [16, 8], P('dp'), may hold values from 0 to 2, as said below
- norm1_gain: float32 [1024], replicated, may hold values from 0.5 to 1.5
- w_in: bfloat16 [1024, 6144], P('dp', 'tensor'), may hold values from -0.1875 to 0.1875
- w_decay: bfloat16 [1024, 16], P('dp', 'tensor'), may hold values from -0.1875 to 0.1875
- conv_w: bfloat16 [8, 2048], P('tensor', 'dp'), may hold values from -4 to 4
- decay_log: float32 [8], replicated, may hold values from 0 to 2.5
- decay_bias: float32 [8], replicated, may hold values from -8 to 1
- out_gain: float32 [256], replicated, may hold values from 0.5 to 1.5
- w_out: bfloat16 [2048, 1024], P('tensor', 'dp'), may hold values from -0.25 to 0.25
- norm2_gain: float32 [1024], replicated, may hold values from 0.5 to 1.5
- w_gate: bfloat16 [1024, 2816], P('dp', 'tensor'), may hold values from -0.1875 to 0.1875
- w_up: bfloat16 [1024, 2816], P('dp', 'tensor'), may hold values from -0.1875 to 0.1875
- w_down: bfloat16 [2816, 1024], P('tensor', 'dp'), may hold values from -0.21875 to 0.21875
- cotangent: bfloat16 [8192, 1024], P(('dp', 'tensor')), may hold values from -6 to 6
Outputs:
- out: bfloat16 [8192, 1024], P(('dp', 'tensor'))
- grad_tokens: float32 [8192, 1024], P(('dp', 'tensor'))
- grad_norm1_gain: float32 [1024], replicated
- grad_w_in: float32 [1024, 6144], P('dp', 'tensor')
- grad_w_decay: float32 [1024, 16], P('dp', 'tensor')
- grad_conv_w: float32 [8, 2048], P('tensor', 'dp')
- grad_decay_log: float32 [8], replicated
- grad_decay_bias: float32 [8], replicated
- grad_out_gain: float32 [256], replicated
- grad_w_out: float32 [2048, 1024], P('tensor', 'dp')
- grad_norm2_gain: float32 [1024], replicated
- grad_w_gate: float32 [1024, 2816], P('dp', 'tensor')
- grad_w_up: float32 [1024, 2816], P('dp', 'tensor')
- grad_w_down: float32 [2816, 1024], P('tensor', 'dp')
The draws below stay inside these ranges and needn't reach their ends.
Inputs may be any that keep to these rules, and one draw needn't show every extreme that they name: `block_kind`: per dp index, block j covers tokens j * 64 to (j + 1) * 64 - 1 of its 512. 1: a sequence begins there; 0: the sequence goes on; 2: padding, which only follows all live blocks. Block 0 is 1. At least half of each index's blocks are live and one index is fully live. Each index's first sequence has min(512, live tokens) tokens, no sequence more than 512.
All inputs are finite; a program needn't handle non-finite values.
Results may differ from the reference program's by a relative error of at most 0.019.
Values may be sent and summed in bfloat16 or wider, within the bound.
A program may use at most 192 MiB of HBM per device.

```python
import jax
import jax.numpy as jnp
from jax import lax

D = 1024
H = 8
DK = 128
DV = 256
FF = 2816
BLOCK_LEN = 64
GROUP_TOKENS = 512
SEQ_MAX = 512
TOKENS = 8192
N_DP = 16


def draw_block_kind(key, part):
    key = jax.random.fold_in(key, 7)
    live_key, full_key, start_key = jax.random.split(key, 3)
    per_group = GROUP_TOKENS // BLOCK_LEN
    longest = SEQ_MAX // BLOCK_LEN
    live_count = jax.random.randint(live_key, (N_DP,), (per_group + 1) // 2, per_group + 1)
    full_group = jax.random.randint(full_key, (), 0, N_DP)
    live_count = jnp.where(jnp.arange(N_DP) == full_group, per_group, live_count)
    random_start = jax.random.randint(start_key, (per_group, N_DP), 0, 3) == 0

    def advance(run_length, inputs):
        position, chance = inputs
        begins = (position == 0) | chance & (position >= longest) | (run_length >= longest)
        run_length = jnp.where(begins, 1, run_length + 1)
        kind_now = jnp.where(position >= live_count, 2, begins.astype(jnp.int32))
        return (run_length, kind_now)
    initial_run = jnp.zeros((N_DP,), jnp.int32)
    final_run, kinds = lax.scan(advance, initial_run, (jnp.arange(per_group), random_start))
    return jnp.transpose(kinds).astype(jnp.int32)


def draw_decay_log(key, part):
    key = jax.random.fold_in(key, 11)
    return jax.random.uniform(key, (H,), jnp.float32, 0.0, 2.5)


def draw_decay_bias(key, part):
    key = jax.random.fold_in(key, 13)
    return jax.random.uniform(key, (H,), jnp.float32, -8.0, 1.0)


def block_levels(own_key, shape, shards, smallest, high):
    def one(axis_at, shards_of):
        steps = jax.random.uniform(jax.random.fold_in(jax.random.fold_in(own_key, 6), axis_at), (shards_of,), jnp.float32, smallest / len(shards), high / len(shards))
        return jnp.repeat(jnp.exp(steps), shape[axis_at] // shards_of).reshape((-1,) + (1,) * (len(shape) - axis_at - 1))

    level = one(*shards[0])
    for cut in shards[1:]:
        level = level * one(*cut)
    return level


def bell_draw(key, dims, width, limit, shards=(), held_as=jnp.bfloat16):
    level = block_levels(key, dims, shards, -0.22, 0.18) if shards else 1.0
    values = jax.random.normal(key, dims, jnp.float32) * width * level
    return jnp.minimum(jnp.maximum(values, -limit), limit).astype(held_as)


def setup_inputs(seed: int = 0) -> dict:
    arg_keys = jax.random.split(jax.random.key(seed), 16)
    tokens = bell_draw(arg_keys[0], (TOKENS, D), 1.0, 6.0, ((0, 32),))
    block_kind = draw_block_kind(jax.random.fold_in(arg_keys[15], 71), 0)
    norm1_gain = jnp.clip(1.0 + 0.1 * jax.random.normal(arg_keys[2], (D,), jnp.float32), 0.5, 1.5)
    w_in = bell_draw(arg_keys[3], (D, H * (2 * DK + 2 * DV)), D ** -0.5, 0.1875, ((0, 16), (1, 2)))
    w_decay = bell_draw(arg_keys[4], (D, 2 * H), D ** -0.5, 0.1875, ((0, 16), (1, 2)))
    conv_w = bell_draw(arg_keys[5], (H, 4 * (2 * DK + DV)), 2 ** -0.5, 4.0, ((0, 2), (1, 16)))
    decay_log = draw_decay_log(jax.random.fold_in(arg_keys[15], 71), 0)
    decay_bias = draw_decay_bias(jax.random.fold_in(arg_keys[15], 71), 0)
    out_gain = jnp.clip(1.0 + 0.1 * jax.random.normal(arg_keys[8], (DV,), jnp.float32), 0.5, 1.5)
    w_out = bell_draw(arg_keys[9], (H * DV, D), (H * DV // 4) ** -0.5, 0.25, ((0, 2), (1, 16)))
    norm2_gain = jnp.clip(1.0 + 0.1 * jax.random.normal(arg_keys[10], (D,), jnp.float32), 0.5, 1.5)
    w_gate = bell_draw(arg_keys[11], (D, FF), D ** -0.5, 0.1875, ((0, 16), (1, 2)))
    w_up = bell_draw(arg_keys[12], (D, FF), D ** -0.5, 0.1875, ((0, 16), (1, 2)))
    w_down = bell_draw(arg_keys[13], (FF, D), (FF // 4) ** -0.5, 0.21875, ((0, 2), (1, 16)))
    cotangent = bell_draw(arg_keys[14], (TOKENS, D), 1.0, 6.0, ((0, 32),))
    return {"tokens": tokens, "block_kind": block_kind, "norm1_gain": norm1_gain, "w_in": w_in, "w_decay": w_decay, "conv_w": conv_w, "decay_log": decay_log, "decay_bias": decay_bias, "out_gain": out_gain, "w_out": w_out, "norm2_gain": norm2_gain, "w_gate": w_gate, "w_up": w_up, "w_down": w_down, "cotangent": cotangent}


@jax.custom_vjp
def low(v):
    return lax.optimization_barrier(v.astype(jnp.bfloat16)).astype(jnp.float32)

@jax.custom_vjp
def low_back(v):
    return v

def low_keep(v):
    return (low(v), None)

def low_pass(kept, grad):
    return (grad,)

def back_keep(v):
    return (v, None)

def back_low(kept, grad):
    return (low(grad),)
low.defvjp(low_keep, low_pass)
low_back.defvjp(back_keep, back_low)

def matmul(first_arr, second_arr):
    return jnp.dot(first_arr.astype(jnp.float32), second_arr.astype(jnp.float32), precision=lax.Precision.HIGHEST, preferred_element_type=jnp.float32)

def rms_scale(values, gain):
    return values * lax.rsqrt(lax.optimization_barrier(jnp.mean(values * values, axis=-1, keepdims=True)) + 1e-05) * gain

def live_mask(block_kind):
    count = block_kind.shape[0]
    return jnp.broadcast_to((block_kind != 2)[:, None], (count, BLOCK_LEN)).reshape(count * BLOCK_LEN).astype(jnp.float32)

def block_step(memory_state, inputs):
    query_vecs, key_vecs, value_vecs, log_decay, strength, restart = inputs
    highest = lax.Precision.HIGHEST
    memory_state = memory_state * (1.0 - restart)
    block_len = query_vecs.shape[1]
    cumulative = jnp.cumsum(log_decay, axis=1)
    later = jnp.arange(block_len)[:, None]
    earlier = jnp.arange(block_len)[None, :]
    on_or_below = later >= earlier
    strictly_below = (later > earlier).astype(jnp.float32)
    log_gap = cumulative[:, :, None] - cumulative[:, None, :]
    decay_mat = jnp.exp(jnp.where(on_or_below, log_gap, 0.0)) * on_or_below.astype(jnp.float32)
    keys_dot = jnp.einsum('hid,hjd->hij', key_vecs, key_vecs, precision=highest)
    coupling = strength[:, :, None] * keys_dot * decay_mat * strictly_below
    system = coupling + jnp.eye(block_len, dtype=jnp.float32)
    scaled = jnp.exp(cumulative)
    key_terms = lax.linalg.triangular_solve(system, (strength * scaled)[:, :, None] * key_vecs, left_side=True, lower=True, unit_diagonal=True)
    value_terms = lax.linalg.triangular_solve(system, strength[:, :, None] * value_vecs, left_side=True, lower=True, unit_diagonal=True)
    fresh_values = value_terms - jnp.einsum('hid,hde->hie', key_terms, memory_state, precision=highest)
    scores = jnp.einsum('hid,hjd->hij', query_vecs, key_vecs, precision=highest) * decay_mat
    output = jnp.einsum('hid,hde->hie', query_vecs * scaled[:, :, None], memory_state, precision=highest)
    output = output + jnp.einsum('hij,hje->hie', scores, fresh_values, precision=highest)
    final_log = cumulative[:, -1]
    carried = jnp.exp(final_log)[:, None, None] * memory_state
    carried = carried + jnp.einsum('hid,hie->hde', key_vecs * jnp.exp(final_log[:, None] - cumulative)[:, :, None], fresh_values, precision=highest)
    return (carried, output)

def mix_tokens(projected, decay_in, conv_taps, decay_log, decay_bias, out_gain, block_kind):
    token_count = projected.shape[0]
    head_count = decay_in.shape[1] // 2
    per_head = projected.reshape(token_count, head_count, 2 * DK + 2 * DV)
    conv_in = per_head[:, :, :2 * DK + DV]
    gate_vals = per_head[:, :, 2 * DK + DV:]
    tap_table = conv_taps.reshape(head_count, 4, 2 * DK + DV)
    block_count = token_count // BLOCK_LEN
    begins = (block_kind == 1).astype(jnp.float32)
    first_block = jnp.broadcast_to(begins[:, None], (block_count, BLOCK_LEN)).reshape(token_count)
    offsets = jnp.arange(token_count) % BLOCK_LEN
    conv_out = conv_in * tap_table[None, :, 0, :]
    for lag_count in range(1, 4):
        shifted = jnp.pad(conv_in, ((lag_count, 0), (0, 0), (0, 0)))[:token_count]
        allowed = 1.0 - first_block * (offsets < lag_count).astype(jnp.float32)
        conv_out = conv_out + shifted * tap_table[None, :, lag_count, :] * allowed[:, None, None]
    active = jax.nn.silu(conv_out)
    query_vecs = active[:, :, :DK]
    query_vecs = query_vecs * lax.rsqrt(lax.optimization_barrier(jnp.sum(query_vecs * query_vecs, axis=-1, keepdims=True)) + 1e-06) * DK ** (-0.5)
    key_vecs = active[:, :, DK:2 * DK]
    key_vecs = key_vecs * lax.rsqrt(lax.optimization_barrier(jnp.sum(key_vecs * key_vecs, axis=-1, keepdims=True)) + 1e-06)
    value_vecs = active[:, :, 2 * DK:]
    decay_pair = decay_in.reshape(token_count, head_count, 2)
    log_decay = -jnp.exp(decay_log) * jax.nn.softplus(decay_pair[:, :, 0] + decay_bias)
    strength = jax.nn.sigmoid(decay_pair[:, :, 1])

    def blocked(values):
        return jnp.swapaxes(values.reshape((block_count, BLOCK_LEN) + values.shape[1:]), 1, 2)
    initial = jnp.zeros((head_count, DK, DV), jnp.float32)
    final_state, outputs = lax.scan(jax.checkpoint(block_step), initial, (blocked(query_vecs), blocked(key_vecs), blocked(value_vecs), blocked(log_decay), blocked(strength), begins))
    outputs = jnp.swapaxes(outputs, 1, 2).reshape(token_count, head_count, DV)
    normed = outputs * lax.rsqrt(lax.optimization_barrier(jnp.mean(outputs * outputs, axis=-1, keepdims=True)) + 1e-05) * out_gain * jax.nn.silu(gate_vals)
    return normed.reshape(token_count, head_count * DV)

def block_forward(values, block_kind, norm1_gain, w_in, w_decay, conv_w, decay_log, decay_bias, out_gain, w_out, norm2_gain, w_gate, w_up, w_down):
    normed_in = low(rms_scale(values, norm1_gain))
    projected = low_back(matmul(normed_in, w_in))
    decay_in = low_back(matmul(normed_in, w_decay))
    mixed_out = low(mix_tokens(projected, decay_in, conv_w, decay_log, decay_bias, out_gain, block_kind))
    attn_out = low_back(matmul(mixed_out, w_out))
    residual = values + attn_out
    normed_mid = low(rms_scale(residual, norm2_gain))
    pre_gate = low_back(matmul(normed_mid, w_gate))
    pre_up = low_back(matmul(normed_mid, w_up))
    hidden = low(jax.nn.silu(pre_gate) * pre_up)
    ffn_out = low_back(matmul(hidden, w_down))
    return live_mask(block_kind)[:, None] * (residual + ffn_out)

def reference(tokens, block_kind, norm1_gain, w_in, w_decay, conv_w, decay_log, decay_bias, out_gain, w_out, norm2_gain, w_gate, w_up, w_down, cotangent):
    parameters = tuple((weight.astype(jnp.float32) for weight in (norm1_gain, w_in, w_decay, conv_w, decay_log, decay_bias, out_gain, w_out, norm2_gain, w_gate, w_up, w_down)))
    grouped = tokens.astype(jnp.float32).reshape(N_DP, GROUP_TOKENS, D)
    grouped_grad = cotangent.astype(jnp.float32).reshape(N_DP, GROUP_TOKENS, D)

    def one_group(totals, inputs):
        values, kinds, grad_rows = inputs

        def forward(values_in, *weights):
            return block_forward(values_in, kinds, *weights)
        result, backward = jax.vjp(forward, values, *parameters)
        gradients = backward(grad_rows)
        totals = tuple((total + part_grad for total, part_grad in zip(totals, gradients[1:])))
        return (totals, (result.astype(jnp.bfloat16), gradients[0]))
    initial_sums = tuple((jnp.zeros_like(weight) for weight in parameters))
    totals, (results, input_grads) = lax.scan(one_group, initial_sums, (grouped, block_kind, grouped_grad))
    return (results.reshape(TOKENS, D), input_grads.reshape(TOKENS, D), totals[0], totals[1], totals[2], totals[3], totals[4], totals[5], totals[6], totals[7], totals[8], totals[9], totals[10], totals[11])
```

```python
import functools

import jax
import jax.numpy as jnp
from jax import lax
from jax.experimental import pallas as pl
from jax.experimental.pallas import tpu as pltpu
from jax.sharding import PartitionSpec as P

H = 8
DK = 128
DV = 256
BLOCK_LEN = 64
SEG = 256
VMEM_BYTES = 48 * 1024 * 1024


def rms_scale(values, gain):
    return values * lax.rsqrt(jnp.mean(values * values, axis=-1, keepdims=True) + 1e-05) * gain


def live_mask(block_kind):
    count = block_kind.shape[0]
    return (
        jnp.broadcast_to((block_kind != 2)[:, None], (count, BLOCK_LEN))
        .reshape(count * BLOCK_LEN)
        .astype(jnp.float32)
    )


def contract(first_arr, second_arr, first_dim, second_dim):
    return lax.dot_general(
        first_arr,
        second_arr,
        (((first_dim,), (second_dim,)), ((), ())),
        preferred_element_type=jnp.float32,
    )


def swiglu(pre_gate, pre_up):
    return jax.nn.silu(pre_gate) * pre_up


def mm(first_arr, second_arr, first_dim=1, second_dim=0):
    return lax.dot_general(
        first_arr.astype(jnp.bfloat16),
        second_arr.astype(jnp.bfloat16),
        (((first_dim,), (second_dim,)), ((), ())),
        preferred_element_type=jnp.float32,
    )


def row_sum(values):
    return jnp.sum(values, axis=1, keepdims=True)


def col_sum(values):
    return jnp.sum(values, axis=0, keepdims=True)


def block_iotas():
    rows = lax.broadcasted_iota(jnp.int32, (BLOCK_LEN, BLOCK_LEN), 0)
    cols = lax.broadcasted_iota(jnp.int32, (BLOCK_LEN, BLOCK_LEN), 1)
    return rows, cols


def lag_mask(first_col, seg, lag):
    offsets = lax.broadcasted_iota(jnp.int32, (seg, 1), 0) % BLOCK_LEN
    return 1.0 - first_col * (offsets < lag).astype(jnp.float32)


def conv_part(halo_ref, proj_ref, tap_ref, first_col, padded, seg):
    padded[0:8, :] = halo_ref[:, : 2 * DK + DV]
    padded[8 : 8 + seg, :] = proj_ref[:, : 2 * DK + DV]
    conv = padded[8 : 8 + seg, :] * tap_ref[0, 0:1, :]
    for lag in range(1, 4):
        conv = conv + padded[8 - lag : 8 - lag + seg, :] * tap_ref[0, lag : lag + 1, :] * lag_mask(
            first_col, seg, lag
        )
    return conv


def qkv_part(active):
    query_act = active[:, :DK]
    key_act = active[:, DK : 2 * DK]
    query_inv = lax.rsqrt(row_sum(query_act * query_act) + 1e-06)
    key_inv = lax.rsqrt(row_sum(key_act * key_act) + 1e-06)
    query_vecs = query_act * query_inv * DK ** (-0.5)
    key_vecs = key_act * key_inv
    return query_vecs, key_vecs, active[:, 2 * DK :], query_inv, key_inv


def decay_part(log_decay):
    rows, cols = block_iotas()
    cum_row = col_sum(jnp.where(rows <= cols, log_decay, 0.0))
    cum_col = row_sum(jnp.where(rows == cols, cum_row, 0.0))
    last = cum_row[:, BLOCK_LEN - 1 :]
    decay_mat = jnp.where(rows >= cols, jnp.exp(jnp.where(rows >= cols, cum_col - cum_row, 0.0)), 0.0)
    return cum_col, last, decay_mat


def inverses(couplings):
    rows, cols = block_iotas()
    eye = (rows == cols).astype(jnp.float32)
    results = None
    width = 1
    while width < BLOCK_LEN:
        pair = (rows // (2 * width) == cols // (2 * width)) & (rows // width != cols // width)
        parts = [jnp.where(pair, c, 0.0) for c in couplings]
        if results is None:
            results = [eye - p for p in parts]
        else:
            firsts = [mm(r, p) for r, p in zip(results, parts)]
            results = [r - mm(f, r) for r, f in zip(results, firsts)]
        width *= 2
    return results


def mixer_fwd_kernel(
    seg,
    halo_ref,
    proj_ref,
    tap_ref,
    cols_ref,
    gain_ref,
    mixed_ref,
    inv_ref,
    terms_ref,
    fresh_ref,
    state_ref,
    rec_ref,
    padded,
    carry,
):
    @pl.when(pl.program_id(1) == 0)
    def _():
        carry[...] = jnp.zeros_like(carry)

    first_col = cols_ref[0, :, 2:3]
    conv = conv_part(halo_ref, proj_ref, tap_ref, first_col, padded, seg)
    active = conv * jax.nn.sigmoid(conv)
    query_vecs, key_vecs, value_vecs, _, _ = qkv_part(active)
    rows, cols = block_iotas()
    count = seg // BLOCK_LEN
    at = [slice(n * BLOCK_LEN, (n + 1) * BLOCK_LEN) for n in range(count)]
    beta = [cols_ref[0, s, 1:2] for s in at]
    decays = [decay_part(cols_ref[0, s, 0:1]) for s in at]
    scaled = [jnp.exp(d[0]) for d in decays]
    couplings = [
        jnp.where(rows > cols, b * mm(key_vecs[s], key_vecs[s], 1, 1) * d[2], 0.0)
        for s, b, d in zip(at, beta, decays)
    ]
    inv = inverses(couplings)
    terms = [
        mm(x, jnp.concatenate([b * e * key_vecs[s], b * value_vecs[s]], axis=1))
        for x, b, e, s in zip(inv, beta, scaled, at)
    ]
    scores = [mm(query_vecs[s], key_vecs[s], 1, 1) * d[2] for s, d in zip(at, decays)]
    state = carry[...]
    for n in range(count):
        s = at[n]
        cum_col, last, _ = decays[n]
        state = state * (1.0 - first_col[n * BLOCK_LEN : n * BLOCK_LEN + 1, :])
        state_low = state.astype(jnp.bfloat16)
        fresh = terms[n][:, DK:] - mm(terms[n][:, :DK], state_low)
        out = mm(query_vecs[s] * scaled[n], state_low) + mm(scores[n], fresh)
        rec_ref[0, s, :] = out
        fresh_ref[0, s, :] = fresh.astype(jnp.bfloat16)
        state_ref[0, n * DK : (n + 1) * DK, :] = state_low
        inv_ref[0, s, :] = inv[n].astype(jnp.bfloat16)
        terms_ref[0, s, :] = terms[n].astype(jnp.bfloat16)
        state = jnp.exp(last) * state + mm(key_vecs[s] * jnp.exp(last - cum_col), fresh, 0, 0)
    carry[...] = state
    out = rec_ref[0]
    gate = proj_ref[:, 2 * DK + DV :]
    normed = out * lax.rsqrt(jnp.mean(out * out, axis=1, keepdims=True) + 1e-05)
    mixed_ref[...] = (normed * gain_ref[...] * (gate * jax.nn.sigmoid(gate))).astype(jnp.bfloat16)


def mixer_bwd_kernel(
    seg,
    halo_ref,
    proj_ref,
    tap_ref,
    cols_ref,
    gain_ref,
    inv_ref,
    terms_ref,
    fresh_ref,
    state_ref,
    rec_ref,
    dmix_ref,
    dproj_ref,
    dcols_ref,
    dtap_ref,
    dgain_ref,
    padded,
    carry,
    shifted,
    later,
    dqkv,
):
    wide = 2 * DK + DV

    @pl.when(pl.program_id(1) == 0)
    def _():
        carry[...] = jnp.zeros_like(carry)
        later[...] = jnp.zeros_like(later)
        dtap_ref[...] = jnp.zeros_like(dtap_ref)
        dgain_ref[...] = jnp.zeros_like(dgain_ref)

    first_col = cols_ref[0, :, 2:3]
    conv = conv_part(halo_ref, proj_ref, tap_ref, first_col, padded, seg)
    sig = jax.nn.sigmoid(conv)
    active = conv * sig
    query_vecs, key_vecs, value_vecs, query_inv, key_inv = qkv_part(active)
    rows, cols = block_iotas()
    count = seg // BLOCK_LEN
    at = [slice(n * BLOCK_LEN, (n + 1) * BLOCK_LEN) for n in range(count)]

    out = rec_ref[0]
    gate = proj_ref[:, wide:]
    d_mixed = dmix_ref[...]
    gate_sig = jax.nn.sigmoid(gate)
    inv_rms = lax.rsqrt(jnp.mean(out * out, axis=1, keepdims=True) + 1e-05)
    normed = out * inv_rms
    gated = d_mixed * (gate * gate_sig)
    dgain_ref[0] += col_sum(gated * normed)
    d_normed = gated * gain_ref[...]
    dproj_ref[:, wide:] = (
        d_mixed * normed * gain_ref[...] * gate_sig * (1.0 + gate * (1.0 - gate_sig))
    ).astype(jnp.bfloat16)
    d_out = inv_rms * (d_normed - normed * jnp.mean(d_normed * normed, axis=1, keepdims=True))

    beta = [cols_ref[0, s, 1:2] for s in at]
    decays = [decay_part(cols_ref[0, s, 0:1]) for s in at]
    scaled = [jnp.exp(d[0]) for d in decays]
    ends = [jnp.exp(d[1] - d[0]) for d in decays]
    keys_dot = [mm(key_vecs[s], key_vecs[s], 1, 1) for s in at]
    scores = [mm(query_vecs[s], key_vecs[s], 1, 1) * d[2] for s, d in zip(at, decays)]
    d_score = [mm(d_out[s], fresh_ref[0, s, :], 1, 1) for s in at]
    d_fresh_own = [mm(sc, d_out[s], 0, 0) for sc, s in zip(scores, at)]
    d_scaled_query = [
        mm(d_out[s], state_ref[0, n * DK : (n + 1) * DK, :], 1, 1) for n, s in enumerate(at)
    ]
    d_state_own = [mm(query_vecs[s] * e, d_out[s], 0, 0) for s, e in zip(at, scaled)]
    d_state = carry[...]
    d_fresh = [None] * count
    d_end_key = [None] * count
    d_last = [None] * count
    for n in reversed(range(count)):
        s = at[n]
        low = d_state.astype(jnp.bfloat16)
        fresh = d_fresh_own[n] + mm(key_vecs[s] * ends[n], low)
        d_fresh[n] = fresh
        d_end_key[n] = mm(fresh_ref[0, s, :], low, 1, 1)
        whole = jnp.exp(decays[n][1])
        state = state_ref[0, n * DK : (n + 1) * DK, :].astype(jnp.float32)
        d_last[n] = whole * row_sum(col_sum(d_state * state))
        d_state = d_state_own[n] + whole * d_state - mm(terms_ref[0, s, :DK], fresh, 0, 0)
        d_state = d_state * (1.0 - first_col[n * BLOCK_LEN : n * BLOCK_LEN + 1, :])
    carry[...] = d_state
    d_key_terms = [
        -mm(f, state_ref[0, n * DK : (n + 1) * DK, :], 1, 1) for n, f in enumerate(d_fresh)
    ]
    d_rhs = [
        mm(inv_ref[0, s, :], jnp.concatenate([dk, f], axis=1), 0, 0)
        for s, dk, f in zip(at, d_key_terms, d_fresh)
    ]
    d_coupling = [
        jnp.where(rows > cols, -mm(r, terms_ref[0, s, :], 1, 1), 0.0) for r, s in zip(d_rhs, at)
    ]
    for n in range(count):
        s = at[n]
        b, e, end = beta[n], scaled[n], ends[n]
        decay_mat = decays[n][2]
        query, key, value = query_vecs[s], key_vecs[s], value_vecs[s]
        d_kb = d_rhs[n][:, :DK]
        d_vb = d_rhs[n][:, DK:]
        kb_dot = row_sum(d_kb * key)
        weighted = d_coupling[n] * keys_dot[n] * decay_mat
        d_beta = kb_dot * e + row_sum(d_vb * value) + row_sum(weighted)
        d_log = weighted * b + d_score[n] * scores[n]
        d_keys_dot = d_coupling[n] * b * decay_mat
        d_qk = d_score[n] * decay_mat
        d_query = mm(d_qk, key) + d_scaled_query[n] * e
        d_key = (
            mm(d_keys_dot, key)
            + mm(d_keys_dot, key, 0, 0)
            + mm(d_qk, query, 0, 0)
            + d_kb * (b * e)
            + d_end_key[n] * end
        )
        d_end = row_sum(d_end_key[n] * key) * end
        d_cum = (kb_dot * b + row_sum(d_scaled_query[n] * query)) * e - d_end + row_sum(d_log)
        cum_row = col_sum(jnp.where(rows == cols, d_cum, 0.0) - d_log)
        total = d_last[n] + col_sum(d_end)
        d_log_decay = row_sum(jnp.where(cols >= rows, cum_row, 0.0)) + total
        dcols_ref[0, s, 0:1] = d_log_decay
        dcols_ref[0, s, 1:2] = d_beta
        dqkv[s, :DK] = (
            d_query * (DK ** (-0.5) * query_inv[s])
            - active[s, :DK] * (query_inv[s] * query_inv[s] * row_sum(d_query * query))
        )
        dqkv[s, DK : 2 * DK] = d_key * key_inv[s] - active[s, DK : 2 * DK] * (
            key_inv[s] * key_inv[s] * row_sum(d_key * key)
        )
        dqkv[s, 2 * DK :] = d_vb * b
    d_conv = dqkv[...] * (sig * (1.0 + conv * (1.0 - sig)))
    dtap_ref[0, 0:1, :] += col_sum(d_conv * padded[8 : 8 + seg, :])
    d_in = d_conv * tap_ref[0, 0:1, :]
    for lag in range(1, 4):
        allowed = d_conv * lag_mask(first_col, seg, lag)
        dtap_ref[0, lag : lag + 1, :] += col_sum(allowed * padded[8 - lag : 8 - lag + seg, :])
        shifted[0:seg, :] = allowed * tap_ref[0, lag : lag + 1, :]
        shifted[seg : seg + 8, :] = later[lag - 1]
        d_in = d_in + shifted[lag : lag + seg, :]
        later[lag - 1] = shifted[0:8, :]
    dproj_ref[:, :wide] = d_in.astype(jnp.bfloat16)


def mixer_specs(count, seg, back):
    def seg_at(s):
        return count - 1 - s if back else s

    wide = 2 * DK + 2 * DV
    return [
        pl.BlockSpec((8, wide), lambda h, s: (jnp.maximum(seg_at(s) * (seg // 8) - 1, 0), h)),
        pl.BlockSpec((seg, wide), lambda h, s: (seg_at(s), h)),
        pl.BlockSpec((1, 4, 2 * DK + DV), lambda h, s: (h, 0, 0)),
        pl.BlockSpec((1, seg, 4), lambda h, s: (h, seg_at(s), 0)),
        pl.BlockSpec((1, DV), lambda h, s: (0, 0)),
    ], [
        pl.BlockSpec((1, seg, BLOCK_LEN), lambda h, s: (h, seg_at(s), 0)),
        pl.BlockSpec((1, seg, DK + DV), lambda h, s: (h, seg_at(s), 0)),
        pl.BlockSpec((1, seg, DV), lambda h, s: (h, seg_at(s), 0)),
        pl.BlockSpec((1, seg // BLOCK_LEN * DK, DV), lambda h, s: (h, seg_at(s), 0)),
        pl.BlockSpec((1, seg, DV), lambda h, s: (h, seg_at(s), 0)),
    ], pl.BlockSpec((seg, DV), lambda h, s: (seg_at(s), h))


def mixer_forward(projected, taps, cols, gain):
    tokens = projected.shape[0]
    heads = taps.shape[0]
    seg = min(SEG, tokens)
    count = tokens // seg
    ins, saved, mix = mixer_specs(count, seg, False)
    low = jnp.bfloat16
    return pl.pallas_call(
        functools.partial(mixer_fwd_kernel, seg),
        grid=(heads, count),
        in_specs=ins,
        out_specs=[mix] + saved,
        out_shape=[
            jax.ShapeDtypeStruct((tokens, heads * DV), low),
            jax.ShapeDtypeStruct((heads, tokens, BLOCK_LEN), low),
            jax.ShapeDtypeStruct((heads, tokens, DK + DV), low),
            jax.ShapeDtypeStruct((heads, tokens, DV), low),
            jax.ShapeDtypeStruct((heads, tokens // BLOCK_LEN * DK, DV), low),
            jax.ShapeDtypeStruct((heads, tokens, DV), jnp.float32),
        ],
        scratch_shapes=[
            pltpu.VMEM((seg + 8, 2 * DK + DV), jnp.float32),
            pltpu.VMEM((DK, DV), jnp.float32),
        ],
        compiler_params=pltpu.CompilerParams(vmem_limit_bytes=VMEM_BYTES),
        cost_estimate=pl.CostEstimate(
            flops=tokens * heads * 1000000, bytes_accessed=tokens * heads * 8000, transcendentals=0
        ),
        name="mixer_forward",
    )(projected, projected, taps, cols, gain)


def mixer_backward(projected, taps, cols, gain, saved_vals, d_mixed):
    tokens = projected.shape[0]
    heads = taps.shape[0]
    seg = min(SEG, tokens)
    count = tokens // seg
    ins, saved, mix = mixer_specs(count, seg, True)
    wide = 2 * DK + DV
    return pl.pallas_call(
        functools.partial(mixer_bwd_kernel, seg),
        grid=(heads, count),
        in_specs=ins + saved + [mix],
        out_specs=[
            ins[1],
            pl.BlockSpec((1, seg, 2), lambda h, s: (h, count - 1 - s, 0)),
            ins[2],
            pl.BlockSpec((1, 1, DV), lambda h, s: (h, 0, 0)),
        ],
        out_shape=[
            jax.ShapeDtypeStruct(projected.shape, jnp.bfloat16),
            jax.ShapeDtypeStruct((heads, tokens, 2), jnp.float32),
            jax.ShapeDtypeStruct(taps.shape, jnp.float32),
            jax.ShapeDtypeStruct((heads, 1, DV), jnp.float32),
        ],
        scratch_shapes=[
            pltpu.VMEM((seg + 8, wide), jnp.float32),
            pltpu.VMEM((DK, DV), jnp.float32),
            pltpu.VMEM((seg + 8, wide), jnp.float32),
            pltpu.VMEM((3, 8, wide), jnp.float32),
            pltpu.VMEM((seg, wide), jnp.float32),
        ],
        compiler_params=pltpu.CompilerParams(vmem_limit_bytes=VMEM_BYTES),
        cost_estimate=pl.CostEstimate(
            flops=tokens * heads * 2000000, bytes_accessed=tokens * heads * 9000, transcendentals=0
        ),
        name="mixer_backward",
    )(projected, projected, taps, cols, gain, *saved_vals, d_mixed)


def decay_columns(decay_in, decay_log, decay_bias):
    pairs = decay_in.reshape(decay_in.shape[0], -1, 2)
    log_decay = -jnp.exp(decay_log) * jax.nn.softplus(pairs[:, :, 0] + decay_bias)
    return log_decay.T, jax.nn.sigmoid(pairs[:, :, 1]).T


def body(
    tokens,
    block_kind,
    norm1_gain,
    w_in,
    w_decay,
    conv_w,
    decay_log,
    decay_bias,
    out_gain,
    w_out,
    norm2_gain,
    w_gate,
    w_up,
    w_down,
    cotangent,
):
    row_count = tokens.shape[0]
    tensor_index = lax.axis_index("tensor")
    heads_here = w_decay.shape[1] // 2
    kinds = block_kind[0]
    full_in, full_decay, full_gate, full_up = (
        lax.all_gather(w_in, "dp", axis=0, tiled=True),
        lax.all_gather(w_decay, "dp", axis=0, tiled=True),
        lax.all_gather(w_gate, "dp", axis=0, tiled=True),
        lax.all_gather(w_up, "dp", axis=0, tiled=True),
    )
    full_out, full_down, conv_here = (
        lax.all_gather(w_out, "dp", axis=1, tiled=True),
        lax.all_gather(w_down, "dp", axis=1, tiled=True),
        lax.all_gather(conv_w, "dp", axis=1, tiled=True),
    )
    decay_here = lax.dynamic_slice_in_dim(decay_log, tensor_index * heads_here, heads_here)
    bias_here = lax.dynamic_slice_in_dim(decay_bias, tensor_index * heads_here, heads_here)
    rows_in = tokens.astype(jnp.float32)
    normed_in, first_norm_back = jax.vjp(rms_scale, rows_in, norm1_gain)
    group_in = lax.all_gather(normed_in.astype(jnp.bfloat16), "tensor", axis=0, tiled=True)
    projected = jnp.dot(group_in, full_in, preferred_element_type=jnp.float32)
    decay_in = jnp.dot(group_in, full_decay, preferred_element_type=jnp.float32)

    (log_decay, strength), decay_back = jax.vjp(decay_columns, decay_in, decay_here, bias_here)
    begins = jnp.broadcast_to(
        jnp.repeat((kinds == 1).astype(jnp.float32), BLOCK_LEN), log_decay.shape
    )
    cols = jnp.stack([log_decay, strength, begins, begins], axis=-1)
    taps = conv_here.astype(jnp.float32).reshape(heads_here, 4, 2 * DK + DV)
    gain_row = out_gain.reshape(1, DV)
    mixed_low, *saved_vals = mixer_forward(projected, taps, cols, gain_row)
    attn_out = lax.psum_scatter(
        jnp.dot(mixed_low, full_out, preferred_element_type=jnp.float32),
        "tensor",
        scatter_dimension=0,
        tiled=True,
    )
    residual = rows_in + attn_out
    normed_mid, second_norm_back = jax.vjp(rms_scale, residual, norm2_gain)
    mid_low = normed_mid.astype(jnp.bfloat16)
    live_here = lax.dynamic_slice_in_dim(live_mask(kinds), tensor_index * row_count, row_count)
    grad_out = live_here[:, None] * cotangent.astype(jnp.float32)
    grad_low = grad_out.astype(jnp.bfloat16)
    group_mid = lax.all_gather(mid_low, "tensor", axis=0, tiled=True)
    pre_gate = jnp.dot(group_mid, full_gate, preferred_element_type=jnp.float32)
    pre_up = jnp.dot(group_mid, full_up, preferred_element_type=jnp.float32)
    hidden, swiglu_back = jax.vjp(swiglu, pre_gate, pre_up)
    hidden_low = hidden.astype(jnp.bfloat16)
    ffn_out = lax.psum_scatter(
        jnp.dot(hidden_low, full_down, preferred_element_type=jnp.float32).astype(jnp.bfloat16),
        "tensor",
        scatter_dimension=0,
        tiled=True,
    ).astype(jnp.float32)
    grad_group = lax.all_gather(grad_low, "tensor", axis=0, tiled=True)
    d_hidden = contract(grad_group, full_down, 1, 1)
    grad_down = contract(hidden_low, grad_group, 0, 0)
    d_gate, d_up = swiglu_back(d_hidden)
    d_gate_low = d_gate.astype(jnp.bfloat16)
    d_up_low = d_up.astype(jnp.bfloat16)
    grad_gate = contract(group_mid, d_gate_low, 0, 0)
    grad_up = contract(group_mid, d_up_low, 0, 0)
    d_mid = lax.psum_scatter(
        contract(d_gate_low, full_gate, 1, 1) + contract(d_up_low, full_up, 1, 1),
        "tensor",
        scatter_dimension=0,
        tiled=True,
    )
    out = (live_here[:, None] * (residual + ffn_out)).astype(jnp.bfloat16)
    d_resid_norm, grad_gain_mid = second_norm_back(d_mid)
    d_residual = grad_out + d_resid_norm
    attn_group = lax.all_gather(d_residual.astype(jnp.bfloat16), "tensor", axis=0, tiled=True)
    d_mixed = contract(attn_group, full_out, 1, 1)
    grad_outw = contract(mixed_low, attn_group, 0, 0)
    d_proj_low, d_cols, d_taps, d_gain_heads = mixer_backward(
        projected, taps, cols, gain_row, saved_vals, d_mixed
    )
    d_decay_in, d_decay, d_bias = decay_back((d_cols[:, :, 0], d_cols[:, :, 1]))
    d_taps = d_taps.reshape(heads_here, -1)
    d_out_gain = jnp.sum(d_gain_heads, axis=(0, 1))
    d_decay_low = d_decay_in.astype(jnp.bfloat16)
    grad_inw = contract(group_in, d_proj_low, 0, 0)
    grad_decayw = contract(group_in, d_decay_low, 0, 0)
    d_in = lax.psum_scatter(
        (contract(d_proj_low, full_in, 1, 1) + contract(d_decay_low, full_decay, 1, 1)).astype(
            jnp.bfloat16
        ),
        "tensor",
        scatter_dimension=0,
        tiled=True,
    ).astype(jnp.float32)
    d_rows_norm, grad_gain_in = first_norm_back(d_in)
    grad_tokens = d_residual + d_rows_norm
    row_grads = (
        lax.psum_scatter(
            grad_inw.astype(jnp.bfloat16), "dp", scatter_dimension=0, tiled=True
        ).astype(jnp.float32),
        lax.psum_scatter(
            grad_decayw.astype(jnp.bfloat16), "dp", scatter_dimension=0, tiled=True
        ).astype(jnp.float32),
        lax.psum_scatter(
            grad_gate.astype(jnp.bfloat16), "dp", scatter_dimension=0, tiled=True
        ).astype(jnp.float32),
        lax.psum_scatter(
            grad_up.astype(jnp.bfloat16), "dp", scatter_dimension=0, tiled=True
        ).astype(jnp.float32),
    )
    col_grads = (
        lax.psum_scatter(
            grad_outw.astype(jnp.bfloat16), "dp", scatter_dimension=1, tiled=True
        ).astype(jnp.float32),
        lax.psum_scatter(
            grad_down.astype(jnp.bfloat16), "dp", scatter_dimension=1, tiled=True
        ).astype(jnp.float32),
        lax.psum_scatter(d_taps.astype(jnp.bfloat16), "dp", scatter_dimension=1, tiled=True).astype(
            jnp.float32
        ),
    )
    decay_full = lax.dynamic_update_slice_in_dim(
        jnp.zeros((H,), jnp.float32), d_decay, tensor_index * heads_here, 0
    )
    bias_full = lax.dynamic_update_slice_in_dim(
        jnp.zeros((H,), jnp.float32), d_bias, tensor_index * heads_here, 0
    )
    small_sums = lax.psum(
        (grad_gain_in, grad_gain_mid, d_out_gain, decay_full, bias_full), ("dp", "tensor")
    )
    return (
        out,
        grad_tokens,
        small_sums[0],
        row_grads[0],
        row_grads[1],
        col_grads[2],
        small_sums[3],
        small_sums[4],
        small_sums[2],
        col_grads[0],
        small_sums[1],
        row_grads[2],
        row_grads[3],
        col_grads[1],
    )


def solution(mesh):
    in_specs = (
        P(("dp", "tensor"), None),
        P("dp", None),
        P(),
        P("dp", "tensor"),
        P("dp", "tensor"),
        P("tensor", "dp"),
        P(),
        P(),
        P(),
        P("tensor", "dp"),
        P(),
        P("dp", "tensor"),
        P("dp", "tensor"),
        P("tensor", "dp"),
        P(("dp", "tensor"), None),
    )
    out_specs = (
        P(("dp", "tensor"), None),
        P(("dp", "tensor"), None),
        P(),
        P("dp", "tensor"),
        P("dp", "tensor"),
        P("tensor", "dp"),
        P(),
        P(),
        P(),
        P("tensor", "dp"),
        P(),
        P("dp", "tensor"),
        P("dp", "tensor"),
        P("tensor", "dp"),
    )
    return jax.shard_map(body, mesh=mesh, in_specs=in_specs, out_specs=out_specs, check_vma=False)
```

```python
import functools

import jax
import jax.numpy as jnp
from jax import lax
from jax.experimental import pallas as pl
from jax.experimental.pallas import tpu as pltpu
from jax.sharding import PartitionSpec as P

H = 8
DK = 128
DV = 256
BLOCK_LEN = 64
SEG = 256
VMEM_BYTES = 48 * 1024 * 1024


def rms_scale(values, gain):
    return values * lax.rsqrt(jnp.mean(values * values, axis=-1, keepdims=True) + 1e-05) * gain


def live_mask(block_kind):
    count = block_kind.shape[0]
    return (
        jnp.broadcast_to((block_kind != 2)[:, None], (count, BLOCK_LEN))
        .reshape(count * BLOCK_LEN)
        .astype(jnp.float32)
    )


def contract(first_arr, second_arr, first_dim, second_dim):
    return lax.dot_general(
        first_arr,
        second_arr,
        (((first_dim,), (second_dim,)), ((), ())),
        preferred_element_type=jnp.float32,
    )


def swiglu(pre_gate, pre_up):
    return jax.nn.silu(pre_gate) * pre_up


def mm(first_arr, second_arr, first_dim=1, second_dim=0):
    return lax.dot_general(
        first_arr.astype(jnp.bfloat16),
        second_arr.astype(jnp.bfloat16),
        (((first_dim,), (second_dim,)), ((), ())),
        preferred_element_type=jnp.float32,
    )


def row_sum(values):
    return jnp.sum(values, axis=1, keepdims=True)


def col_sum(values):
    return jnp.sum(values, axis=0, keepdims=True)


def block_iotas():
    rows = lax.broadcasted_iota(jnp.int32, (BLOCK_LEN, BLOCK_LEN), 0)
    cols = lax.broadcasted_iota(jnp.int32, (BLOCK_LEN, BLOCK_LEN), 1)
    return rows, cols


def lag_mask(first_col, seg, lag):
    offsets = lax.broadcasted_iota(jnp.int32, (seg, 1), 0) % BLOCK_LEN
    return 1.0 - first_col * (offsets < lag).astype(jnp.float32)


def conv_part(halo_ref, proj_ref, tap_ref, first_col, padded, seg):
    padded[0:8, :] = halo_ref[:, : 2 * DK + DV]
    padded[8 : 8 + seg, :] = proj_ref[:, : 2 * DK + DV]
    conv = padded[8 : 8 + seg, :] * tap_ref[0, 0:1, :]
    for lag in range(1, 4):
        conv = conv + padded[8 - lag : 8 - lag + seg, :] * tap_ref[0, lag : lag + 1, :] * lag_mask(
            first_col, seg, lag
        )
    return conv


def qkv_part(active):
    query_act = active[:, :DK]
    key_act = active[:, DK : 2 * DK]
    query_inv = lax.rsqrt(row_sum(query_act * query_act) + 1e-06)
    key_inv = lax.rsqrt(row_sum(key_act * key_act) + 1e-06)
    query_vecs = query_act * query_inv * DK ** (-0.5)
    key_vecs = key_act * key_inv
    return query_vecs, key_vecs, active[:, 2 * DK :], query_inv, key_inv


def decay_part(log_decay):
    rows, cols = block_iotas()
    cum_row = col_sum(jnp.where(rows <= cols, log_decay, 0.0))
    cum_col = row_sum(jnp.where(rows == cols, cum_row, 0.0))
    last = cum_row[:, BLOCK_LEN - 1 :]
    decay_mat = jnp.where(rows >= cols, jnp.exp(jnp.where(rows >= cols, cum_col - cum_row, 0.0)), 0.0)
    return cum_col, last, decay_mat


def inverses(couplings):
    rows, cols = block_iotas()
    eye = (rows == cols).astype(jnp.float32)
    results = None
    width = 1
    while width < BLOCK_LEN:
        pair = (rows // (2 * width) == cols // (2 * width)) & (rows // width != cols // width)
        parts = [jnp.where(pair, c, 0.0) for c in couplings]
        if results is None:
            results = [eye - p for p in parts]
        else:
            firsts = [mm(r, p) for r, p in zip(results, parts)]
            results = [r - mm(f, r) for r, f in zip(results, firsts)]
        width *= 2
    return results


def mixer_fwd_kernel(
    seg,
    halo_ref,
    proj_ref,
    tap_ref,
    cols_ref,
    gain_ref,
    mixed_ref,
    inv_ref,
    terms_ref,
    fresh_ref,
    state_ref,
    rec_ref,
    padded,
    carry,
):
    @pl.when(pl.program_id(1) == 0)
    def _():
        carry[...] = jnp.zeros_like(carry)

    first_col = cols_ref[0, :, 2:3]
    conv = conv_part(halo_ref, proj_ref, tap_ref, first_col, padded, seg)
    active = conv * jax.nn.sigmoid(conv)
    query_vecs, key_vecs, value_vecs, _, _ = qkv_part(active)
    rows, cols = block_iotas()
    count = seg // BLOCK_LEN
    at = [slice(n * BLOCK_LEN, (n + 1) * BLOCK_LEN) for n in range(count)]
    beta = [cols_ref[0, s, 1:2] for s in at]
    decays = [decay_part(cols_ref[0, s, 0:1]) for s in at]
    scaled = [jnp.exp(d[0]) for d in decays]
    couplings = [
        jnp.where(rows > cols, b * mm(key_vecs[s], key_vecs[s], 1, 1) * d[2], 0.0)
        for s, b, d in zip(at, beta, decays)
    ]
    inv = inverses(couplings)
    terms = [
        mm(x, jnp.concatenate([b * e * key_vecs[s], b * value_vecs[s]], axis=1))
        for x, b, e, s in zip(inv, beta, scaled, at)
    ]
    scores = [mm(query_vecs[s], key_vecs[s], 1, 1) * d[2] for s, d in zip(at, decays)]
    state = carry[...]
    for n in range(count):
        s = at[n]
        cum_col, last, _ = decays[n]
        state = state * (1.0 - first_col[n * BLOCK_LEN : n * BLOCK_LEN + 1, :])
        state_low = state.astype(jnp.bfloat16)
        fresh = terms[n][:, DK:] - mm(terms[n][:, :DK], state_low)
        out = mm(query_vecs[s] * scaled[n], state_low) + mm(scores[n], fresh)
        rec_ref[0, s, :] = out
        fresh_ref[0, s, :] = fresh.astype(jnp.bfloat16)
        state_ref[0, n * DK : (n + 1) * DK, :] = state_low
        inv_ref[0, s, :] = inv[n].astype(jnp.bfloat16)
        terms_ref[0, s, :] = terms[n].astype(jnp.bfloat16)
        state = jnp.exp(last) * state + mm(key_vecs[s] * jnp.exp(last - cum_col), fresh, 0, 0)
    carry[...] = state
    out = rec_ref[0]
    gate = proj_ref[:, 2 * DK + DV :]
    normed = out * lax.rsqrt(jnp.mean(out * out, axis=1, keepdims=True) + 1e-05)
    mixed_ref[...] = (normed * gain_ref[...] * (gate * jax.nn.sigmoid(gate))).astype(jnp.bfloat16)


def mixer_bwd_kernel(
    seg,
    halo_ref,
    proj_ref,
    tap_ref,
    cols_ref,
    gain_ref,
    inv_ref,
    terms_ref,
    fresh_ref,
    state_ref,
    rec_ref,
    dmix_ref,
    dproj_ref,
    dcols_ref,
    dtap_ref,
    dgain_ref,
    padded,
    carry,
    shifted,
    later,
    dqkv,
):
    wide = 2 * DK + DV

    @pl.when(pl.program_id(1) == 0)
    def _():
        carry[...] = jnp.zeros_like(carry)
        later[...] = jnp.zeros_like(later)
        dtap_ref[...] = jnp.zeros_like(dtap_ref)
        dgain_ref[...] = jnp.zeros_like(dgain_ref)

    first_col = cols_ref[0, :, 2:3]
    conv = conv_part(halo_ref, proj_ref, tap_ref, first_col, padded, seg)
    sig = jax.nn.sigmoid(conv)
    active = conv * sig
    query_vecs, key_vecs, value_vecs, query_inv, key_inv = qkv_part(active)
    rows, cols = block_iotas()
    count = seg // BLOCK_LEN
    at = [slice(n * BLOCK_LEN, (n + 1) * BLOCK_LEN) for n in range(count)]

    out = rec_ref[0]
    gate = proj_ref[:, wide:]
    d_mixed = dmix_ref[...]
    gate_sig = jax.nn.sigmoid(gate)
    inv_rms = lax.rsqrt(jnp.mean(out * out, axis=1, keepdims=True) + 1e-05)
    normed = out * inv_rms
    gated = d_mixed * (gate * gate_sig)
    dgain_ref[0] += col_sum(gated * normed)
    d_normed = gated * gain_ref[...]
    dproj_ref[:, wide:] = (
        d_mixed * normed * gain_ref[...] * gate_sig * (1.0 + gate * (1.0 - gate_sig))
    ).astype(jnp.bfloat16)
    d_out = inv_rms * (d_normed - normed * jnp.mean(d_normed * normed, axis=1, keepdims=True))

    beta = [cols_ref[0, s, 1:2] for s in at]
    decays = [decay_part(cols_ref[0, s, 0:1]) for s in at]
    scaled = [jnp.exp(d[0]) for d in decays]
    ends = [jnp.exp(d[1] - d[0]) for d in decays]
    keys_dot = [mm(key_vecs[s], key_vecs[s], 1, 1) for s in at]
    scores = [mm(query_vecs[s], key_vecs[s], 1, 1) * d[2] for s, d in zip(at, decays)]
    d_score = [mm(d_out[s], fresh_ref[0, s, :], 1, 1) for s in at]
    d_fresh_own = [mm(sc, d_out[s], 0, 0) for sc, s in zip(scores, at)]
    d_scaled_query = [
        mm(d_out[s], state_ref[0, n * DK : (n + 1) * DK, :], 1, 1) for n, s in enumerate(at)
    ]
    d_state_own = [mm(query_vecs[s] * e, d_out[s], 0, 0) for s, e in zip(at, scaled)]
    d_state = carry[...]
    d_fresh = [None] * count
    d_end_key = [None] * count
    d_last = [None] * count
    for n in reversed(range(count)):
        s = at[n]
        low = d_state.astype(jnp.bfloat16)
        fresh = d_fresh_own[n] + mm(key_vecs[s] * ends[n], low)
        d_fresh[n] = fresh
        d_end_key[n] = mm(fresh_ref[0, s, :], low, 1, 1)
        whole = jnp.exp(decays[n][1])
        state = state_ref[0, n * DK : (n + 1) * DK, :].astype(jnp.float32)
        d_last[n] = whole * row_sum(col_sum(d_state * state))
        d_state = d_state_own[n] + whole * d_state - mm(terms_ref[0, s, :DK], fresh, 0, 0)
        d_state = d_state * (1.0 - first_col[n * BLOCK_LEN : n * BLOCK_LEN + 1, :])
    carry[...] = d_state
    d_key_terms = [
        -mm(f, state_ref[0, n * DK : (n + 1) * DK, :], 1, 1) for n, f in enumerate(d_fresh)
    ]
    d_rhs = [
        mm(inv_ref[0, s, :], jnp.concatenate([dk, f], axis=1), 0, 0)
        for s, dk, f in zip(at, d_key_terms, d_fresh)
    ]
    d_coupling = [
        jnp.where(rows > cols, -mm(r, terms_ref[0, s, :], 1, 1), 0.0) for r, s in zip(d_rhs, at)
    ]
    for n in range(count):
        s = at[n]
        b, e, end = beta[n], scaled[n], ends[n]
        decay_mat = decays[n][2]
        query, key, value = query_vecs[s], key_vecs[s], value_vecs[s]
        d_kb = d_rhs[n][:, :DK]
        d_vb = d_rhs[n][:, DK:]
        kb_dot = row_sum(d_kb * key)
        weighted = d_coupling[n] * keys_dot[n] * decay_mat
        d_beta = kb_dot * e + row_sum(d_vb * value) + row_sum(weighted)
        d_log = weighted * b + d_score[n] * scores[n]
        d_keys_dot = d_coupling[n] * b * decay_mat
        d_qk = d_score[n] * decay_mat
        d_query = mm(d_qk, key) + d_scaled_query[n] * e
        d_key = (
            mm(d_keys_dot, key)
            + mm(d_keys_dot, key, 0, 0)
            + mm(d_qk, query, 0, 0)
            + d_kb * (b * e)
            + d_end_key[n] * end
        )
        d_end = row_sum(d_end_key[n] * key) * end
        d_cum = (kb_dot * b + row_sum(d_scaled_query[n] * query)) * e - d_end + row_sum(d_log)
        cum_row = col_sum(jnp.where(rows == cols, d_cum, 0.0) - d_log)
        total = d_last[n] + col_sum(d_end)
        d_log_decay = row_sum(jnp.where(cols >= rows, cum_row, 0.0)) + total
        dcols_ref[0, s, 0:1] = d_log_decay
        dcols_ref[0, s, 1:2] = d_beta
        dqkv[s, :DK] = (
            d_query * (DK ** (-0.5) * query_inv[s])
            - active[s, :DK] * (query_inv[s] * query_inv[s] * row_sum(d_query * query))
        )
        dqkv[s, DK : 2 * DK] = d_key * key_inv[s] - active[s, DK : 2 * DK] * (
            key_inv[s] * key_inv[s] * row_sum(d_key * key)
        )
        dqkv[s, 2 * DK :] = d_vb * b
    d_conv = dqkv[...] * (sig * (1.0 + conv * (1.0 - sig)))
    dtap_ref[0, 0:1, :] += col_sum(d_conv * padded[8 : 8 + seg, :])
    d_in = d_conv * tap_ref[0, 0:1, :]
    for lag in range(1, 4):
        allowed = d_conv * lag_mask(first_col, seg, lag)
        dtap_ref[0, lag : lag + 1, :] += col_sum(allowed * padded[8 - lag : 8 - lag + seg, :])
        shifted[0:seg, :] = allowed * tap_ref[0, lag : lag + 1, :]
        shifted[seg : seg + 8, :] = later[lag - 1]
        d_in = d_in + shifted[lag : lag + seg, :]
        later[lag - 1] = shifted[0:8, :]
    dproj_ref[:, :wide] = d_in.astype(jnp.bfloat16)


def mixer_specs(count, seg, back):
    def seg_at(s):
        return count - 1 - s if back else s

    wide = 2 * DK + 2 * DV
    return [
        pl.BlockSpec((8, wide), lambda h, s: (jnp.maximum(seg_at(s) * (seg // 8) - 1, 0), h)),
        pl.BlockSpec((seg, wide), lambda h, s: (seg_at(s), h)),
        pl.BlockSpec((1, 4, 2 * DK + DV), lambda h, s: (h, 0, 0)),
        pl.BlockSpec((1, seg, 4), lambda h, s: (h, seg_at(s), 0)),
        pl.BlockSpec((1, DV), lambda h, s: (0, 0)),
    ], [
        pl.BlockSpec((1, seg, BLOCK_LEN), lambda h, s: (h, seg_at(s), 0)),
        pl.BlockSpec((1, seg, DK + DV), lambda h, s: (h, seg_at(s), 0)),
        pl.BlockSpec((1, seg, DV), lambda h, s: (h, seg_at(s), 0)),
        pl.BlockSpec((1, seg // BLOCK_LEN * DK, DV), lambda h, s: (h, seg_at(s), 0)),
        pl.BlockSpec((1, seg, DV), lambda h, s: (h, seg_at(s), 0)),
    ], pl.BlockSpec((seg, DV), lambda h, s: (seg_at(s), h))


def mixer_forward(projected, taps, cols, gain):
    tokens = projected.shape[0]
    heads = taps.shape[0]
    seg = min(SEG, tokens)
    count = tokens // seg
    ins, saved, mix = mixer_specs(count, seg, False)
    low = jnp.bfloat16
    return pl.pallas_call(
        functools.partial(mixer_fwd_kernel, seg),
        grid=(heads, count),
        in_specs=ins,
        out_specs=[mix] + saved,
        out_shape=[
            jax.ShapeDtypeStruct((tokens, heads * DV), low),
            jax.ShapeDtypeStruct((heads, tokens, BLOCK_LEN), low),
            jax.ShapeDtypeStruct((heads, tokens, DK + DV), low),
            jax.ShapeDtypeStruct((heads, tokens, DV), low),
            jax.ShapeDtypeStruct((heads, tokens // BLOCK_LEN * DK, DV), low),
            jax.ShapeDtypeStruct((heads, tokens, DV), jnp.float32),
        ],
        scratch_shapes=[
            pltpu.VMEM((seg + 8, 2 * DK + DV), jnp.float32),
            pltpu.VMEM((DK, DV), jnp.float32),
        ],
        compiler_params=pltpu.CompilerParams(vmem_limit_bytes=VMEM_BYTES),
        cost_estimate=pl.CostEstimate(
            flops=tokens * heads * 1000000, bytes_accessed=tokens * heads * 8000, transcendentals=0
        ),
        name="mixer_forward",
    )(projected, projected, taps, cols, gain)


def mixer_backward(projected, taps, cols, gain, saved_vals, d_mixed):
    tokens = projected.shape[0]
    heads = taps.shape[0]
    seg = min(SEG, tokens)
    count = tokens // seg
    ins, saved, mix = mixer_specs(count, seg, True)
    wide = 2 * DK + DV
    return pl.pallas_call(
        functools.partial(mixer_bwd_kernel, seg),
        grid=(heads, count),
        in_specs=ins + saved + [mix],
        out_specs=[
            ins[1],
            pl.BlockSpec((1, seg, 2), lambda h, s: (h, count - 1 - s, 0)),
            ins[2],
            pl.BlockSpec((1, 1, DV), lambda h, s: (h, 0, 0)),
        ],
        out_shape=[
            jax.ShapeDtypeStruct(projected.shape, jnp.bfloat16),
            jax.ShapeDtypeStruct((heads, tokens, 2), jnp.float32),
            jax.ShapeDtypeStruct(taps.shape, jnp.float32),
            jax.ShapeDtypeStruct((heads, 1, DV), jnp.float32),
        ],
        scratch_shapes=[
            pltpu.VMEM((seg + 8, wide), jnp.float32),
            pltpu.VMEM((DK, DV), jnp.float32),
            pltpu.VMEM((seg + 8, wide), jnp.float32),
            pltpu.VMEM((3, 8, wide), jnp.float32),
            pltpu.VMEM((seg, wide), jnp.float32),
        ],
        compiler_params=pltpu.CompilerParams(vmem_limit_bytes=VMEM_BYTES),
        cost_estimate=pl.CostEstimate(
            flops=tokens * heads * 2000000, bytes_accessed=tokens * heads * 9000, transcendentals=0
        ),
        name="mixer_backward",
    )(projected, projected, taps, cols, gain, *saved_vals, d_mixed)


def decay_columns(decay_in, decay_log, decay_bias):
    pairs = decay_in.reshape(decay_in.shape[0], -1, 2)
    log_decay = -jnp.exp(decay_log) * jax.nn.softplus(pairs[:, :, 0] + decay_bias)
    return log_decay.T, jax.nn.sigmoid(pairs[:, :, 1]).T


def plane_swap(values, size, flip):
    return lax.ppermute(values, "dp", [(i, i ^ flip) for i in range(size)])


def outer_shift(values, size, step):
    return lax.ppermute(values, "dp", [(i, (i + 4 * step) % size) for i in range(size)])


def dp_position():
    index = lax.axis_index("dp")
    return index // 4, (index // 2) % 2, index % 2


def gather_dp(block):
    size = lax.axis_size("dp")
    outer = size // 4
    depth, width = block.shape
    half = width // 256 * 128
    at_z, at_y, at_x = dp_position()
    column = jnp.zeros((outer, depth, width), block.dtype)
    column = lax.dynamic_update_slice(column, block[None], (at_z, 0, 0))
    for step in range(1, outer):
        got = outer_shift(block, size, step)
        column = lax.dynamic_update_slice(column, got[None], ((at_z - step) % outer, 0, 0))
    from_x = plane_swap(column, size, 1)
    from_y = plane_swap(column, size, 2)
    low = plane_swap(from_x[:, :, :half], size, 2)
    high = plane_swap(from_y[:, :, half:], size, 1)
    full = jnp.zeros((outer, 2, 2, depth, width), block.dtype)

    def put(whole, part, row, col, start):
        return lax.dynamic_update_slice(whole, part[:, None, None], (0, row, col, 0, start))

    full = put(full, column, at_y, at_x, 0)
    full = put(full, from_x, at_y, 1 - at_x, 0)
    full = put(full, from_y, 1 - at_y, at_x, 0)
    full = put(full, low, 1 - at_y, 1 - at_x, 0)
    full = put(full, high, 1 - at_y, 1 - at_x, half)
    return full.reshape(size * depth, width)


def scatter_dp(whole):
    size = lax.axis_size("dp")
    outer = size // 4
    depth = whole.shape[0] // size
    width = whole.shape[1]
    half = width // 256 * 128
    at_z, at_y, at_x = dp_position()
    parts = whole.reshape(outer, 2, 2, depth, width)

    def pick(values, axis, index):
        return lax.dynamic_index_in_dim(values, index, axis, keepdims=False)

    def add(first, second):
        return (first.astype(jnp.float32) + second.astype(jnp.float32)).astype(jnp.bfloat16)

    low, high = parts[..., :half], parts[..., half:]
    got_low = plane_swap(pick(low, 1, 1 - at_y), size, 2)
    got_high = plane_swap(pick(high, 2, 1 - at_x), size, 1)
    low = add(pick(low, 1, at_y), got_low)
    high = add(pick(high, 2, at_x), got_high)
    got_low = plane_swap(pick(low, 1, 1 - at_x), size, 1)
    got_high = plane_swap(pick(high, 1, 1 - at_y), size, 2)
    low = add(pick(low, 1, at_x), got_low)
    high = add(pick(high, 1, at_y), got_high)
    column = jnp.concatenate([low, high], axis=2)
    total = pick(column, 0, at_z).astype(jnp.float32)
    for step in range(1, outer):
        sent = pick(column, 0, (at_z + step) % outer)
        total = total + outer_shift(sent, size, step).astype(jnp.float32)
    return total


def sum_all(values):
    size = lax.axis_size("dp")
    outer = size // 4
    at_z = dp_position()[0]
    values = lax.psum(values, "tensor")
    values = values + plane_swap(values, size, 1)
    values = values + plane_swap(values, size, 2)
    table = jnp.zeros((outer,) + values.shape, values.dtype)
    table = lax.dynamic_update_slice(table, values[None], (at_z, 0))
    for step in range(1, outer):
        got = outer_shift(values, size, step)
        table = lax.dynamic_update_slice(table, got[None], ((at_z - step) % outer, 0))
    return jnp.sum(table, axis=0)


def pad_to(values, rows, cols):
    return jnp.pad(values, ((0, rows - values.shape[0]), (0, cols - values.shape[1])))


def body(
    tokens,
    block_kind,
    norm1_gain,
    w_in,
    w_decay,
    conv_w,
    decay_log,
    decay_bias,
    out_gain,
    w_out,
    norm2_gain,
    w_gate,
    w_up,
    w_down,
    cotangent,
):
    row_count = tokens.shape[0]
    tensor_index = lax.axis_index("tensor")
    heads_here = w_decay.shape[1] // 2
    kinds = block_kind[0]
    depth, in_width = w_in.shape
    ffn_width = w_gate.shape[1]
    out_width = w_out.shape[0]
    dp_size = lax.axis_size("dp")
    decay_width = w_decay.shape[1]
    tap_width = conv_w.shape[1] * heads_here
    tap_pad = -(-tap_width // depth // 128) * 128
    taps_flat = pad_to(conv_w.reshape(depth, tap_width // depth), depth, tap_pad)
    first_pack = gather_dp(
        jnp.concatenate([w_in, pad_to(w_decay, depth, 128), taps_flat], axis=1)
    )
    full_in = first_pack[:, :in_width]
    full_decay = first_pack[:, in_width : in_width + decay_width]
    conv_here = (
        first_pack[:, in_width + 128 : in_width + 128 + tap_width // depth]
        .reshape(dp_size, heads_here, conv_w.shape[1])
        .swapaxes(0, 1)
        .reshape(heads_here, -1)
    )
    second_pack = gather_dp(jnp.concatenate([w_out.T, w_gate, w_up, w_down.T], axis=1))
    starts = [0, out_width, out_width + ffn_width, out_width + 2 * ffn_width]
    full_out = second_pack[:, : starts[1]].T
    full_gate = second_pack[:, starts[1] : starts[2]]
    full_up = second_pack[:, starts[2] : starts[3]]
    full_down = second_pack[:, starts[3] :].T
    decay_here = lax.dynamic_slice_in_dim(decay_log, tensor_index * heads_here, heads_here)
    bias_here = lax.dynamic_slice_in_dim(decay_bias, tensor_index * heads_here, heads_here)
    rows_in = tokens.astype(jnp.float32)
    normed_in, first_norm_back = jax.vjp(rms_scale, rows_in, norm1_gain)
    group_in = lax.all_gather(normed_in.astype(jnp.bfloat16), "tensor", axis=0, tiled=True)
    projected = jnp.dot(group_in, full_in, preferred_element_type=jnp.float32)
    decay_in = jnp.dot(group_in, full_decay, preferred_element_type=jnp.float32)

    (log_decay, strength), decay_back = jax.vjp(decay_columns, decay_in, decay_here, bias_here)
    begins = jnp.broadcast_to(
        jnp.repeat((kinds == 1).astype(jnp.float32), BLOCK_LEN), log_decay.shape
    )
    cols = jnp.stack([log_decay, strength, begins, begins], axis=-1)
    taps = conv_here.astype(jnp.float32).reshape(heads_here, 4, 2 * DK + DV)
    gain_row = out_gain.reshape(1, DV)
    mixed_low, *saved_vals = mixer_forward(projected, taps, cols, gain_row)
    attn_out = lax.psum_scatter(
        jnp.dot(mixed_low, full_out, preferred_element_type=jnp.float32),
        "tensor",
        scatter_dimension=0,
        tiled=True,
    )
    residual = rows_in + attn_out
    normed_mid, second_norm_back = jax.vjp(rms_scale, residual, norm2_gain)
    mid_low = normed_mid.astype(jnp.bfloat16)
    live_here = lax.dynamic_slice_in_dim(live_mask(kinds), tensor_index * row_count, row_count)
    grad_out = live_here[:, None] * cotangent.astype(jnp.float32)
    grad_low = grad_out.astype(jnp.bfloat16)
    group_mid = lax.all_gather(mid_low, "tensor", axis=0, tiled=True)
    pre_gate = jnp.dot(group_mid, full_gate, preferred_element_type=jnp.float32)
    pre_up = jnp.dot(group_mid, full_up, preferred_element_type=jnp.float32)
    hidden, swiglu_back = jax.vjp(swiglu, pre_gate, pre_up)
    hidden_low = hidden.astype(jnp.bfloat16)
    ffn_out = lax.psum_scatter(
        jnp.dot(hidden_low, full_down, preferred_element_type=jnp.float32).astype(jnp.bfloat16),
        "tensor",
        scatter_dimension=0,
        tiled=True,
    ).astype(jnp.float32)
    grad_group = lax.all_gather(grad_low, "tensor", axis=0, tiled=True)
    d_hidden = contract(grad_group, full_down, 1, 1)
    d_gate, d_up = swiglu_back(d_hidden)
    d_gate_low = d_gate.astype(jnp.bfloat16)
    d_up_low = d_up.astype(jnp.bfloat16)
    grad_gate = contract(group_mid, d_gate_low, 0, 0)
    grad_up = contract(group_mid, d_up_low, 0, 0)
    d_mid = lax.psum_scatter(
        contract(d_gate_low, full_gate, 1, 1) + contract(d_up_low, full_up, 1, 1),
        "tensor",
        scatter_dimension=0,
        tiled=True,
    )
    out = (live_here[:, None] * (residual + ffn_out)).astype(jnp.bfloat16)
    d_resid_norm, grad_gain_mid = second_norm_back(d_mid)
    d_residual = grad_out + d_resid_norm
    attn_group = lax.all_gather(d_residual.astype(jnp.bfloat16), "tensor", axis=0, tiled=True)
    d_mixed = contract(attn_group, full_out, 1, 1)
    d_proj_low, d_cols, d_taps, d_gain_heads = mixer_backward(
        projected, taps, cols, gain_row, saved_vals, d_mixed
    )
    d_decay_in, d_decay, d_bias = decay_back((d_cols[:, :, 0], d_cols[:, :, 1]))
    d_taps = d_taps.reshape(heads_here, -1)
    d_out_gain = jnp.sum(d_gain_heads, axis=(0, 1))
    d_decay_low = d_decay_in.astype(jnp.bfloat16)
    grad_inw = contract(group_in, d_proj_low, 0, 0)
    grad_decayw = contract(group_in, d_decay_low, 0, 0)
    d_in = lax.psum_scatter(
        (contract(d_proj_low, full_in, 1, 1) + contract(d_decay_low, full_decay, 1, 1)).astype(
            jnp.bfloat16
        ),
        "tensor",
        scatter_dimension=0,
        tiled=True,
    ).astype(jnp.float32)
    d_rows_norm, grad_gain_in = first_norm_back(d_in)
    grad_tokens = d_residual + d_rows_norm
    low = jnp.bfloat16
    second_sum = scatter_dp(
        jnp.concatenate(
            [contract(attn_group, mixed_low, 0, 0).astype(low), grad_gate.astype(low),
             grad_up.astype(low), contract(grad_group, hidden_low, 0, 0).astype(low)],
            axis=1,
        )
    )
    tap_rows = (
        d_taps.astype(low)
        .reshape(heads_here, dp_size, conv_w.shape[1])
        .swapaxes(0, 1)
        .reshape(dp_size * depth, tap_width // depth)
    )
    first_sum = scatter_dp(
        jnp.concatenate(
            [grad_inw.astype(low), pad_to(grad_decayw.astype(low), dp_size * depth, 128),
             pad_to(tap_rows, dp_size * depth, tap_pad)],
            axis=1,
        )
    )
    row_grads = (
        first_sum[:, :in_width],
        first_sum[:, in_width : in_width + decay_width],
        second_sum[:, starts[1] : starts[2]],
        second_sum[:, starts[2] : starts[3]],
    )
    col_grads = (
        second_sum[:, : starts[1]].T,
        second_sum[:, starts[3] :].T,
        first_sum[:, in_width + 128 : in_width + 128 + tap_width // depth].reshape(conv_w.shape),
    )
    decay_full = lax.dynamic_update_slice_in_dim(
        jnp.zeros((H,), jnp.float32), d_decay, tensor_index * heads_here, 0
    )
    bias_full = lax.dynamic_update_slice_in_dim(
        jnp.zeros((H,), jnp.float32), d_bias, tensor_index * heads_here, 0
    )
    sizes = [grad_gain_in.shape[0], grad_gain_mid.shape[0], DV, H, H]
    ends = [sum(sizes[: i + 1]) for i in range(5)]
    joined = jnp.concatenate([grad_gain_in, grad_gain_mid, d_out_gain, decay_full, bias_full])
    joined = sum_all(jnp.pad(joined, (0, -ends[4] % 128)))
    small_sums = [joined[e - s : e] for s, e in zip(sizes, ends)]
    return (
        out,
        grad_tokens,
        small_sums[0],
        row_grads[0],
        row_grads[1],
        col_grads[2],
        small_sums[3],
        small_sums[4],
        small_sums[2],
        col_grads[0],
        small_sums[1],
        row_grads[2],
        row_grads[3],
        col_grads[1],
    )


def solution(mesh):
    in_specs = (
        P(("dp", "tensor"), None),
        P("dp", None),
        P(),
        P("dp", "tensor"),
        P("dp", "tensor"),
        P("tensor", "dp"),
        P(),
        P(),
        P(),
        P("tensor", "dp"),
        P(),
        P("dp", "tensor"),
        P("dp", "tensor"),
        P("tensor", "dp"),
        P(("dp", "tensor"), None),
    )
    out_specs = (
        P(("dp", "tensor"), None),
        P(("dp", "tensor"), None),
        P(),
        P("dp", "tensor"),
        P("dp", "tensor"),
        P("tensor", "dp"),
        P(),
        P(),
        P(),
        P("tensor", "dp"),
        P(),
        P("dp", "tensor"),
        P("dp", "tensor"),
        P("tensor", "dp"),
    )
    return jax.shard_map(body, mesh=mesh, in_specs=in_specs, out_specs=out_specs, check_vma=False)
```

```python
import functools

import jax
import jax.numpy as jnp
from jax import lax
from jax.experimental import pallas as pl
from jax.experimental.pallas import tpu as pltpu
from jax.sharding import PartitionSpec as P

H = 8
DK = 128
DV = 256
BLOCK_LEN = 64
SEG = 256
VMEM_BYTES = 48 * 1024 * 1024


def rms_scale(values, gain):
    return values * lax.rsqrt(jnp.mean(values * values, axis=-1, keepdims=True) + 1e-05) * gain


def live_mask(block_kind):
    count = block_kind.shape[0]
    return (
        jnp.broadcast_to((block_kind != 2)[:, None], (count, BLOCK_LEN))
        .reshape(count * BLOCK_LEN)
        .astype(jnp.float32)
    )


def contract(first_arr, second_arr, first_dim, second_dim):
    return lax.dot_general(
        first_arr,
        second_arr,
        (((first_dim,), (second_dim,)), ((), ())),
        preferred_element_type=jnp.float32,
    )


def swiglu(pre_gate, pre_up):
    return jax.nn.silu(pre_gate) * pre_up


def mm(first_arr, second_arr, first_dim=1, second_dim=0):
    return lax.dot_general(
        first_arr.astype(jnp.bfloat16),
        second_arr.astype(jnp.bfloat16),
        (((first_dim,), (second_dim,)), ((), ())),
        preferred_element_type=jnp.float32,
    )


def row_sum(values):
    return jnp.sum(values, axis=1, keepdims=True)


def col_sum(values):
    return jnp.sum(values, axis=0, keepdims=True)


def block_iotas():
    rows = lax.broadcasted_iota(jnp.int32, (BLOCK_LEN, BLOCK_LEN), 0)
    cols = lax.broadcasted_iota(jnp.int32, (BLOCK_LEN, BLOCK_LEN), 1)
    return rows, cols


def lag_mask(first_col, seg, lag):
    offsets = lax.broadcasted_iota(jnp.int32, (seg, 1), 0) % BLOCK_LEN
    return 1.0 - first_col * (offsets < lag).astype(jnp.float32)


def conv_part(halo_ref, proj_ref, tap_ref, first_col, padded, seg):
    padded[0:8, :] = halo_ref[:, : 2 * DK + DV]
    padded[8 : 8 + seg, :] = proj_ref[:, : 2 * DK + DV]
    conv = padded[8 : 8 + seg, :] * tap_ref[0, 0:1, :]
    for lag in range(1, 4):
        conv = conv + padded[8 - lag : 8 - lag + seg, :] * tap_ref[0, lag : lag + 1, :] * lag_mask(
            first_col, seg, lag
        )
    return conv


def qkv_part(active):
    query_act = active[:, :DK]
    key_act = active[:, DK : 2 * DK]
    query_inv = lax.rsqrt(row_sum(query_act * query_act) + 1e-06)
    key_inv = lax.rsqrt(row_sum(key_act * key_act) + 1e-06)
    query_vecs = query_act * query_inv * DK ** (-0.5)
    key_vecs = key_act * key_inv
    return query_vecs, key_vecs, active[:, 2 * DK :], query_inv, key_inv


def decay_part(log_decay):
    rows, cols = block_iotas()
    cum_row = col_sum(jnp.where(rows <= cols, log_decay, 0.0))
    cum_col = row_sum(jnp.where(rows == cols, cum_row, 0.0))
    last = cum_row[:, BLOCK_LEN - 1 :]
    decay_mat = jnp.where(rows >= cols, jnp.exp(jnp.where(rows >= cols, cum_col - cum_row, 0.0)), 0.0)
    return cum_col, last, decay_mat


def inverses(couplings):
    rows, cols = block_iotas()
    eye = (rows == cols).astype(jnp.float32)
    results = None
    width = 1
    while width < BLOCK_LEN:
        pair = (rows // (2 * width) == cols // (2 * width)) & (rows // width != cols // width)
        parts = [jnp.where(pair, c, 0.0) for c in couplings]
        if results is None:
            results = [eye - p for p in parts]
        else:
            firsts = [mm(r, p) for r, p in zip(results, parts)]
            results = [r - mm(f, r) for r, f in zip(results, firsts)]
        width *= 2
    return results


def mixer_fwd_kernel(
    seg,
    halo_ref,
    proj_ref,
    tap_ref,
    cols_ref,
    gain_ref,
    mixed_ref,
    inv_ref,
    terms_ref,
    fresh_ref,
    state_ref,
    rec_ref,
    padded,
    carry,
):
    @pl.when(pl.program_id(1) == 0)
    def _():
        carry[...] = jnp.zeros_like(carry)

    first_col = cols_ref[0, :, 2:3]
    conv = conv_part(halo_ref, proj_ref, tap_ref, first_col, padded, seg)
    active = conv * jax.nn.sigmoid(conv)
    query_vecs, key_vecs, value_vecs, _, _ = qkv_part(active)
    rows, cols = block_iotas()
    count = seg // BLOCK_LEN
    at = [slice(n * BLOCK_LEN, (n + 1) * BLOCK_LEN) for n in range(count)]
    beta = [cols_ref[0, s, 1:2] for s in at]
    decays = [decay_part(cols_ref[0, s, 0:1]) for s in at]
    scaled = [jnp.exp(d[0]) for d in decays]
    couplings = [
        jnp.where(rows > cols, b * mm(key_vecs[s], key_vecs[s], 1, 1) * d[2], 0.0)
        for s, b, d in zip(at, beta, decays)
    ]
    inv = inverses(couplings)
    terms = [
        mm(x, jnp.concatenate([b * e * key_vecs[s], b * value_vecs[s]], axis=1))
        for x, b, e, s in zip(inv, beta, scaled, at)
    ]
    scores = [mm(query_vecs[s], key_vecs[s], 1, 1) * d[2] for s, d in zip(at, decays)]
    state = carry[...]
    for n in range(count):
        s = at[n]
        cum_col, last, _ = decays[n]
        state = state * (1.0 - first_col[n * BLOCK_LEN : n * BLOCK_LEN + 1, :])
        state_low = state.astype(jnp.bfloat16)
        fresh = terms[n][:, DK:] - mm(terms[n][:, :DK], state_low)
        out = mm(query_vecs[s] * scaled[n], state_low) + mm(scores[n], fresh)
        rec_ref[0, s, :] = out
        fresh_ref[0, s, :] = fresh.astype(jnp.bfloat16)
        state_ref[0, n * DK : (n + 1) * DK, :] = state_low
        inv_ref[0, s, :] = inv[n].astype(jnp.bfloat16)
        terms_ref[0, s, :] = terms[n].astype(jnp.bfloat16)
        state = jnp.exp(last) * state + mm(key_vecs[s] * jnp.exp(last - cum_col), fresh, 0, 0)
    carry[...] = state
    out = rec_ref[0]
    gate = proj_ref[:, 2 * DK + DV :]
    normed = out * lax.rsqrt(jnp.mean(out * out, axis=1, keepdims=True) + 1e-05)
    mixed_ref[...] = (normed * gain_ref[...] * (gate * jax.nn.sigmoid(gate))).astype(jnp.bfloat16)


def mixer_bwd_kernel(
    seg,
    halo_ref,
    proj_ref,
    tap_ref,
    cols_ref,
    gain_ref,
    inv_ref,
    terms_ref,
    fresh_ref,
    state_ref,
    rec_ref,
    dmix_ref,
    dproj_ref,
    dcols_ref,
    dtap_ref,
    dgain_ref,
    padded,
    carry,
    shifted,
    later,
    dqkv,
):
    wide = 2 * DK + DV

    @pl.when(pl.program_id(1) == 0)
    def _():
        carry[...] = jnp.zeros_like(carry)
        later[...] = jnp.zeros_like(later)
        dtap_ref[...] = jnp.zeros_like(dtap_ref)
        dgain_ref[...] = jnp.zeros_like(dgain_ref)

    first_col = cols_ref[0, :, 2:3]
    conv = conv_part(halo_ref, proj_ref, tap_ref, first_col, padded, seg)
    sig = jax.nn.sigmoid(conv)
    active = conv * sig
    query_vecs, key_vecs, value_vecs, query_inv, key_inv = qkv_part(active)
    rows, cols = block_iotas()
    count = seg // BLOCK_LEN
    at = [slice(n * BLOCK_LEN, (n + 1) * BLOCK_LEN) for n in range(count)]

    out = rec_ref[0]
    gate = proj_ref[:, wide:]
    d_mixed = dmix_ref[...]
    gate_sig = jax.nn.sigmoid(gate)
    inv_rms = lax.rsqrt(jnp.mean(out * out, axis=1, keepdims=True) + 1e-05)
    normed = out * inv_rms
    gated = d_mixed * (gate * gate_sig)
    dgain_ref[0] += col_sum(gated * normed)
    d_normed = gated * gain_ref[...]
    dproj_ref[:, wide:] = (
        d_mixed * normed * gain_ref[...] * gate_sig * (1.0 + gate * (1.0 - gate_sig))
    ).astype(jnp.bfloat16)
    d_out = inv_rms * (d_normed - normed * jnp.mean(d_normed * normed, axis=1, keepdims=True))

    beta = [cols_ref[0, s, 1:2] for s in at]
    decays = [decay_part(cols_ref[0, s, 0:1]) for s in at]
    scaled = [jnp.exp(d[0]) for d in decays]
    ends = [jnp.exp(d[1] - d[0]) for d in decays]
    keys_dot = [mm(key_vecs[s], key_vecs[s], 1, 1) for s in at]
    scores = [mm(query_vecs[s], key_vecs[s], 1, 1) * d[2] for s, d in zip(at, decays)]
    d_score = [mm(d_out[s], fresh_ref[0, s, :], 1, 1) for s in at]
    d_fresh_own = [mm(sc, d_out[s], 0, 0) for sc, s in zip(scores, at)]
    d_scaled_query = [
        mm(d_out[s], state_ref[0, n * DK : (n + 1) * DK, :], 1, 1) for n, s in enumerate(at)
    ]
    d_state_own = [mm(query_vecs[s] * e, d_out[s], 0, 0) for s, e in zip(at, scaled)]
    d_state = carry[...]
    d_fresh = [None] * count
    d_end_key = [None] * count
    d_last = [None] * count
    for n in reversed(range(count)):
        s = at[n]
        low = d_state.astype(jnp.bfloat16)
        fresh = d_fresh_own[n] + mm(key_vecs[s] * ends[n], low)
        d_fresh[n] = fresh
        d_end_key[n] = mm(fresh_ref[0, s, :], low, 1, 1)
        whole = jnp.exp(decays[n][1])
        state = state_ref[0, n * DK : (n + 1) * DK, :].astype(jnp.float32)
        d_last[n] = whole * row_sum(col_sum(d_state * state))
        d_state = d_state_own[n] + whole * d_state - mm(terms_ref[0, s, :DK], fresh, 0, 0)
        d_state = d_state * (1.0 - first_col[n * BLOCK_LEN : n * BLOCK_LEN + 1, :])
    carry[...] = d_state
    d_key_terms = [
        -mm(f, state_ref[0, n * DK : (n + 1) * DK, :], 1, 1) for n, f in enumerate(d_fresh)
    ]
    d_rhs = [
        mm(inv_ref[0, s, :], jnp.concatenate([dk, f], axis=1), 0, 0)
        for s, dk, f in zip(at, d_key_terms, d_fresh)
    ]
    d_coupling = [
        jnp.where(rows > cols, -mm(r, terms_ref[0, s, :], 1, 1), 0.0) for r, s in zip(d_rhs, at)
    ]
    for n in range(count):
        s = at[n]
        b, e, end = beta[n], scaled[n], ends[n]
        decay_mat = decays[n][2]
        query, key, value = query_vecs[s], key_vecs[s], value_vecs[s]
        d_kb = d_rhs[n][:, :DK]
        d_vb = d_rhs[n][:, DK:]
        kb_dot = row_sum(d_kb * key)
        weighted = d_coupling[n] * keys_dot[n] * decay_mat
        d_beta = kb_dot * e + row_sum(d_vb * value) + row_sum(weighted)
        d_log = weighted * b + d_score[n] * scores[n]
        d_keys_dot = d_coupling[n] * b * decay_mat
        d_qk = d_score[n] * decay_mat
        d_query = mm(d_qk, key) + d_scaled_query[n] * e
        d_key = (
            mm(d_keys_dot, key)
            + mm(d_keys_dot, key, 0, 0)
            + mm(d_qk, query, 0, 0)
            + d_kb * (b * e)
            + d_end_key[n] * end
        )
        d_end = row_sum(d_end_key[n] * key) * end
        d_cum = (kb_dot * b + row_sum(d_scaled_query[n] * query)) * e - d_end + row_sum(d_log)
        cum_row = col_sum(jnp.where(rows == cols, d_cum, 0.0) - d_log)
        total = d_last[n] + col_sum(d_end)
        d_log_decay = row_sum(jnp.where(cols >= rows, cum_row, 0.0)) + total
        dcols_ref[0, s, 0:1] = d_log_decay
        dcols_ref[0, s, 1:2] = d_beta
        dqkv[s, :DK] = (
            d_query * (DK ** (-0.5) * query_inv[s])
            - active[s, :DK] * (query_inv[s] * query_inv[s] * row_sum(d_query * query))
        )
        dqkv[s, DK : 2 * DK] = d_key * key_inv[s] - active[s, DK : 2 * DK] * (
            key_inv[s] * key_inv[s] * row_sum(d_key * key)
        )
        dqkv[s, 2 * DK :] = d_vb * b
    d_conv = dqkv[...] * (sig * (1.0 + conv * (1.0 - sig)))
    dtap_ref[0, 0:1, :] += col_sum(d_conv * padded[8 : 8 + seg, :])
    d_in = d_conv * tap_ref[0, 0:1, :]
    for lag in range(1, 4):
        allowed = d_conv * lag_mask(first_col, seg, lag)
        dtap_ref[0, lag : lag + 1, :] += col_sum(allowed * padded[8 - lag : 8 - lag + seg, :])
        shifted[0:seg, :] = allowed * tap_ref[0, lag : lag + 1, :]
        shifted[seg : seg + 8, :] = later[lag - 1]
        d_in = d_in + shifted[lag : lag + seg, :]
        later[lag - 1] = shifted[0:8, :]
    dproj_ref[:, :wide] = d_in.astype(jnp.bfloat16)


def mixer_specs(count, seg, back):
    def seg_at(s):
        return count - 1 - s if back else s

    wide = 2 * DK + 2 * DV
    return [
        pl.BlockSpec((8, wide), lambda h, s: (jnp.maximum(seg_at(s) * (seg // 8) - 1, 0), h)),
        pl.BlockSpec((seg, wide), lambda h, s: (seg_at(s), h)),
        pl.BlockSpec((1, 4, 2 * DK + DV), lambda h, s: (h, 0, 0)),
        pl.BlockSpec((1, seg, 4), lambda h, s: (h, seg_at(s), 0)),
        pl.BlockSpec((1, DV), lambda h, s: (0, 0)),
    ], [
        pl.BlockSpec((1, seg, BLOCK_LEN), lambda h, s: (h, seg_at(s), 0)),
        pl.BlockSpec((1, seg, DK + DV), lambda h, s: (h, seg_at(s), 0)),
        pl.BlockSpec((1, seg, DV), lambda h, s: (h, seg_at(s), 0)),
        pl.BlockSpec((1, seg // BLOCK_LEN * DK, DV), lambda h, s: (h, seg_at(s), 0)),
        pl.BlockSpec((1, seg, DV), lambda h, s: (h, seg_at(s), 0)),
    ], pl.BlockSpec((seg, DV), lambda h, s: (seg_at(s), h))


def mixer_forward(projected, taps, cols, gain):
    tokens = projected.shape[0]
    heads = taps.shape[0]
    seg = min(SEG, tokens)
    count = tokens // seg
    ins, saved, mix = mixer_specs(count, seg, False)
    low = jnp.bfloat16
    return pl.pallas_call(
        functools.partial(mixer_fwd_kernel, seg),
        grid=(heads, count),
        in_specs=ins,
        out_specs=[mix] + saved,
        out_shape=[
            jax.ShapeDtypeStruct((tokens, heads * DV), low),
            jax.ShapeDtypeStruct((heads, tokens, BLOCK_LEN), low),
            jax.ShapeDtypeStruct((heads, tokens, DK + DV), low),
            jax.ShapeDtypeStruct((heads, tokens, DV), low),
            jax.ShapeDtypeStruct((heads, tokens // BLOCK_LEN * DK, DV), low),
            jax.ShapeDtypeStruct((heads, tokens, DV), jnp.float32),
        ],
        scratch_shapes=[
            pltpu.VMEM((seg + 8, 2 * DK + DV), jnp.float32),
            pltpu.VMEM((DK, DV), jnp.float32),
        ],
        compiler_params=pltpu.CompilerParams(vmem_limit_bytes=VMEM_BYTES),
        cost_estimate=pl.CostEstimate(
            flops=tokens * heads * 1000000, bytes_accessed=tokens * heads * 8000, transcendentals=0
        ),
        name="mixer_forward",
    )(projected, projected, taps, cols, gain)


def mixer_backward(projected, taps, cols, gain, saved_vals, d_mixed):
    tokens = projected.shape[0]
    heads = taps.shape[0]
    seg = min(SEG, tokens)
    count = tokens // seg
    ins, saved, mix = mixer_specs(count, seg, True)
    wide = 2 * DK + DV
    return pl.pallas_call(
        functools.partial(mixer_bwd_kernel, seg),
        grid=(heads, count),
        in_specs=ins + saved + [mix],
        out_specs=[
            ins[1],
            pl.BlockSpec((1, seg, 2), lambda h, s: (h, count - 1 - s, 0)),
            ins[2],
            pl.BlockSpec((1, 1, DV), lambda h, s: (h, 0, 0)),
        ],
        out_shape=[
            jax.ShapeDtypeStruct(projected.shape, jnp.bfloat16),
            jax.ShapeDtypeStruct((heads, tokens, 2), jnp.float32),
            jax.ShapeDtypeStruct(taps.shape, jnp.float32),
            jax.ShapeDtypeStruct((heads, 1, DV), jnp.float32),
        ],
        scratch_shapes=[
            pltpu.VMEM((seg + 8, wide), jnp.float32),
            pltpu.VMEM((DK, DV), jnp.float32),
            pltpu.VMEM((seg + 8, wide), jnp.float32),
            pltpu.VMEM((3, 8, wide), jnp.float32),
            pltpu.VMEM((seg, wide), jnp.float32),
        ],
        compiler_params=pltpu.CompilerParams(vmem_limit_bytes=VMEM_BYTES),
        cost_estimate=pl.CostEstimate(
            flops=tokens * heads * 2000000, bytes_accessed=tokens * heads * 9000, transcendentals=0
        ),
        name="mixer_backward",
    )(projected, projected, taps, cols, gain, *saved_vals, d_mixed)


def decay_columns(decay_in, decay_log, decay_bias):
    pairs = decay_in.reshape(decay_in.shape[0], -1, 2)
    log_decay = -jnp.exp(decay_log) * jax.nn.softplus(pairs[:, :, 0] + decay_bias)
    return log_decay.T, jax.nn.sigmoid(pairs[:, :, 1]).T


def plane_swap(values, size, flip):
    return lax.ppermute(values, "dp", [(i, i ^ flip) for i in range(size)])


def outer_shift(values, size, step):
    return lax.ppermute(values, "dp", [(i, (i + 4 * step) % size) for i in range(size)])


def dp_position():
    index = lax.axis_index("dp")
    return index // 4, (index // 2) % 2, index % 2


def gather_dp(block, after=()):
    size = lax.axis_size("dp")
    outer = size // 4
    depth, width = block.shape
    half = width // 256 * 128
    at_z, at_y, at_x = dp_position()
    column = jnp.zeros((outer, depth, width), block.dtype)
    column = lax.dynamic_update_slice(column, block[None], (at_z, 0, 0))
    for step in range(1, outer):
        got = outer_shift(block, size, step)
        column = lax.dynamic_update_slice(column, got[None], ((at_z - step) % outer, 0, 0))
    column = lax.optimization_barrier((column, *after))[0]
    from_x = plane_swap(column, size, 1)
    from_y = plane_swap(column, size, 2)
    low = plane_swap(from_x[:, :, :half], size, 2)
    high = plane_swap(from_y[:, :, half:], size, 1)
    full = jnp.zeros((outer, 2, 2, depth, width), block.dtype)

    def put(whole, part, row, col, start):
        return lax.dynamic_update_slice(whole, part[:, None, None], (0, row, col, 0, start))

    full = put(full, column, at_y, at_x, 0)
    full = put(full, from_x, at_y, 1 - at_x, 0)
    full = put(full, from_y, 1 - at_y, at_x, 0)
    full = put(full, low, 1 - at_y, 1 - at_x, 0)
    full = put(full, high, 1 - at_y, 1 - at_x, half)
    return full.reshape(size * depth, width), (low, high)


def scatter_dp(whole, beside=None):
    size = lax.axis_size("dp")
    outer = size // 4
    depth = whole.shape[0] // size
    width = whole.shape[1]
    half = width // 256 * 128
    at_z, at_y, at_x = dp_position()
    parts = whole.reshape(outer, 2, 2, depth, width)

    def pick(values, axis, index):
        return lax.dynamic_index_in_dim(values, index, axis, keepdims=False)

    def add(first, second):
        return (first.astype(jnp.float32) + second.astype(jnp.float32)).astype(jnp.bfloat16)

    low, high = parts[..., :half], parts[..., half:]
    got_low = plane_swap(pick(low, 1, 1 - at_y), size, 2)
    got_high = plane_swap(pick(high, 2, 1 - at_x), size, 1)
    if beside is not None:
        got_low, got_high, beside = lax.optimization_barrier((got_low, got_high, beside))
    low = add(pick(low, 1, at_y), got_low)
    high = add(pick(high, 2, at_x), got_high)
    got_low = plane_swap(pick(low, 1, 1 - at_x), size, 1)
    got_high = plane_swap(pick(high, 1, 1 - at_y), size, 2)
    low = add(pick(low, 1, at_x), got_low)
    high = add(pick(high, 1, at_y), got_high)
    column = jnp.concatenate([low, high], axis=2)
    total = pick(column, 0, at_z).astype(jnp.float32)
    for step in range(1, outer):
        sent = pick(column, 0, (at_z + step) % outer)
        total = total + outer_shift(sent, size, step).astype(jnp.float32)
    return total if beside is None else (total, beside)


def tensor_swap(values):
    return lax.ppermute(values, "tensor", [(0, 1), (1, 0)])


def gather_tensor(values):
    if lax.axis_size("tensor") != 2:
        return lax.all_gather(values, "tensor", axis=0, tiled=True)
    me = lax.axis_index("tensor")
    got = tensor_swap(values)
    first = jnp.where(me == 0, values, got)
    second = jnp.where(me == 0, got, values)
    return jnp.concatenate([first, second], axis=0)


def scatter_tensor(values):
    if lax.axis_size("tensor") != 2:
        return lax.psum_scatter(values, "tensor", scatter_dimension=0, tiled=True).astype(
            jnp.float32
        )
    rows = values.shape[0] // 2
    me = lax.axis_index("tensor")
    got = tensor_swap(lax.dynamic_slice_in_dim(values, (1 - me) * rows, rows))
    own = lax.dynamic_slice_in_dim(values, me * rows, rows)
    return own.astype(jnp.float32) + got.astype(jnp.float32)


def pad_to(values, rows, cols):
    return jnp.pad(values, ((0, rows - values.shape[0]), (0, cols - values.shape[1])))


def body(
    tokens,
    block_kind,
    norm1_gain,
    w_in,
    w_decay,
    conv_w,
    decay_log,
    decay_bias,
    out_gain,
    w_out,
    norm2_gain,
    w_gate,
    w_up,
    w_down,
    cotangent,
):
    row_count = tokens.shape[0]
    tensor_index = lax.axis_index("tensor")
    heads_here = w_decay.shape[1] // 2
    kinds = block_kind[0]
    depth, in_width = w_in.shape
    ffn_width = w_gate.shape[1]
    out_width = w_out.shape[0]
    dp_size = lax.axis_size("dp")
    decay_width = w_decay.shape[1]
    tap_width = conv_w.shape[1] * heads_here
    tap_pad = -(-tap_width // depth // 128) * 128
    taps_flat = pad_to(conv_w.reshape(depth, tap_width // depth), depth, tap_pad)
    first_pack, first_moved = gather_dp(
        jnp.concatenate([w_in, pad_to(w_decay, depth, 128), taps_flat], axis=1)
    )
    full_in = first_pack[:, :in_width]
    full_decay = first_pack[:, in_width : in_width + decay_width]
    conv_here = (
        first_pack[:, in_width + 128 : in_width + 128 + tap_width // depth]
        .reshape(dp_size, heads_here, conv_w.shape[1])
        .swapaxes(0, 1)
        .reshape(heads_here, -1)
    )
    second_pack, second_moved = gather_dp(
        jnp.concatenate([w_out.T, w_gate], axis=1), first_moved
    )
    third_pack, _ = gather_dp(jnp.concatenate([w_up, w_down.T], axis=1), second_moved)
    full_out = second_pack[:, :out_width].T
    full_gate = second_pack[:, out_width:]
    full_up = third_pack[:, :ffn_width]
    full_down = third_pack[:, ffn_width:].T
    decay_here = lax.dynamic_slice_in_dim(decay_log, tensor_index * heads_here, heads_here)
    bias_here = lax.dynamic_slice_in_dim(decay_bias, tensor_index * heads_here, heads_here)
    rows_in = tokens.astype(jnp.float32)
    normed_in, first_norm_back = jax.vjp(rms_scale, rows_in, norm1_gain)
    group_in = gather_tensor(normed_in.astype(jnp.bfloat16))
    projected = jnp.dot(group_in, full_in, preferred_element_type=jnp.float32)
    decay_in = jnp.dot(group_in, full_decay, preferred_element_type=jnp.float32)

    (log_decay, strength), decay_back = jax.vjp(decay_columns, decay_in, decay_here, bias_here)
    begins = jnp.broadcast_to(
        jnp.repeat((kinds == 1).astype(jnp.float32), BLOCK_LEN), log_decay.shape
    )
    cols = jnp.stack([log_decay, strength, begins, begins], axis=-1)
    taps = conv_here.astype(jnp.float32).reshape(heads_here, 4, 2 * DK + DV)
    gain_row = out_gain.reshape(1, DV)
    mixed_low, *saved_vals = mixer_forward(projected, taps, cols, gain_row)
    attn_out = scatter_tensor(
        jnp.dot(mixed_low, full_out, preferred_element_type=jnp.float32)
    )
    residual = rows_in + attn_out
    normed_mid, second_norm_back = jax.vjp(rms_scale, residual, norm2_gain)
    mid_low = normed_mid.astype(jnp.bfloat16)
    live_here = lax.dynamic_slice_in_dim(live_mask(kinds), tensor_index * row_count, row_count)
    grad_out = live_here[:, None] * cotangent.astype(jnp.float32)
    grad_low = grad_out.astype(jnp.bfloat16)
    group_mid = gather_tensor(mid_low)
    pre_gate = jnp.dot(group_mid, full_gate, preferred_element_type=jnp.float32)
    pre_up = jnp.dot(group_mid, full_up, preferred_element_type=jnp.float32)
    hidden, swiglu_back = jax.vjp(swiglu, pre_gate, pre_up)
    hidden_low = hidden.astype(jnp.bfloat16)
    ffn_out = scatter_tensor(
        jnp.dot(hidden_low, full_down, preferred_element_type=jnp.float32).astype(jnp.bfloat16)
    )
    grad_group = gather_tensor(grad_low)
    d_hidden = contract(grad_group, full_down, 1, 1)
    d_gate, d_up = swiglu_back(d_hidden)
    d_gate_low = d_gate.astype(jnp.bfloat16)
    d_up_low = d_up.astype(jnp.bfloat16)
    grad_gate = contract(group_mid, d_gate_low, 0, 0)
    grad_up = contract(group_mid, d_up_low, 0, 0)
    d_mid = scatter_tensor(
        contract(d_gate_low, full_gate, 1, 1) + contract(d_up_low, full_up, 1, 1)
    )
    out = (live_here[:, None] * (residual + ffn_out)).astype(jnp.bfloat16)
    d_resid_norm, grad_gain_mid = second_norm_back(d_mid)
    d_residual = grad_out + d_resid_norm
    attn_group = gather_tensor(d_residual.astype(jnp.bfloat16))
    gate_pack = jnp.concatenate(
        [grad_gate.astype(jnp.bfloat16), grad_up.astype(jnp.bfloat16)], axis=1
    )
    out_pack = jnp.concatenate(
        [
            contract(attn_group, mixed_low, 0, 0).astype(jnp.bfloat16),
            contract(grad_group, hidden_low, 0, 0).astype(jnp.bfloat16),
        ],
        axis=1,
    )
    d_mixed, gate_pack, out_pack = lax.optimization_barrier(
        (contract(attn_group, full_out, 1, 1), gate_pack, out_pack)
    )
    d_proj_low, d_cols, d_taps, d_gain_heads = mixer_backward(
        projected, taps, cols, gain_row, saved_vals, d_mixed
    )
    gate_sum, (d_proj_low, d_cols) = scatter_dp(gate_pack, (d_proj_low, d_cols))
    out_sum = scatter_dp(out_pack)
    d_decay_in, d_decay, d_bias = decay_back((d_cols[:, :, 0], d_cols[:, :, 1]))
    d_taps = d_taps.reshape(heads_here, -1)
    d_out_gain = jnp.sum(d_gain_heads, axis=(0, 1))
    d_decay_low = d_decay_in.astype(jnp.bfloat16)
    grad_inw = contract(group_in, d_proj_low, 0, 0)
    grad_decayw = contract(group_in, d_decay_low, 0, 0)
    d_in = scatter_tensor(
        (contract(d_proj_low, full_in, 1, 1) + contract(d_decay_low, full_decay, 1, 1)).astype(
            jnp.bfloat16
        )
    )
    d_rows_norm, grad_gain_in = first_norm_back(d_in)
    grad_tokens = d_residual + d_rows_norm
    low = jnp.bfloat16
    tap_rows = (
        d_taps.astype(low)
        .reshape(heads_here, dp_size, conv_w.shape[1])
        .swapaxes(0, 1)
        .reshape(dp_size * depth, tap_width // depth)
    )
    first_sum = scatter_dp(
        jnp.concatenate(
            [grad_inw.astype(low), pad_to(grad_decayw.astype(low), dp_size * depth, 128),
             pad_to(tap_rows, dp_size * depth, tap_pad)],
            axis=1,
        )
    )
    row_grads = (
        first_sum[:, :in_width],
        first_sum[:, in_width : in_width + decay_width],
        gate_sum[:, :ffn_width],
        gate_sum[:, ffn_width:],
    )
    col_grads = (
        out_sum[:, :out_width].T,
        out_sum[:, out_width:].T,
        first_sum[:, in_width + 128 : in_width + 128 + tap_width // depth].reshape(conv_w.shape),
    )
    decay_full = lax.dynamic_update_slice_in_dim(
        jnp.zeros((H,), jnp.float32), d_decay, tensor_index * heads_here, 0
    )
    bias_full = lax.dynamic_update_slice_in_dim(
        jnp.zeros((H,), jnp.float32), d_bias, tensor_index * heads_here, 0
    )
    sizes = [grad_gain_in.shape[0], grad_gain_mid.shape[0], DV, H, H]
    ends = [sum(sizes[: i + 1]) for i in range(5)]
    joined = jnp.concatenate([grad_gain_in, grad_gain_mid, d_out_gain, decay_full, bias_full])
    joined = lax.psum(joined, ("dp", "tensor"))
    small_sums = [joined[e - s : e] for s, e in zip(sizes, ends)]
    return (
        out,
        grad_tokens,
        small_sums[0],
        row_grads[0],
        row_grads[1],
        col_grads[2],
        small_sums[3],
        small_sums[4],
        small_sums[2],
        col_grads[0],
        small_sums[1],
        row_grads[2],
        row_grads[3],
        col_grads[1],
    )


def solution(mesh):
    in_specs = (
        P(("dp", "tensor"), None),
        P("dp", None),
        P(),
        P("dp", "tensor"),
        P("dp", "tensor"),
        P("tensor", "dp"),
        P(),
        P(),
        P(),
        P("tensor", "dp"),
        P(),
        P("dp", "tensor"),
        P("dp", "tensor"),
        P("tensor", "dp"),
        P(("dp", "tensor"), None),
    )
    out_specs = (
        P(("dp", "tensor"), None),
        P(("dp", "tensor"), None),
        P(),
        P("dp", "tensor"),
        P("dp", "tensor"),
        P("tensor", "dp"),
        P(),
        P(),
        P(),
        P("tensor", "dp"),
        P(),
        P("dp", "tensor"),
        P("dp", "tensor"),
        P("tensor", "dp"),
    )
    return jax.shard_map(body, mesh=mesh, in_specs=in_specs, out_specs=out_specs, check_vma=False)
```

```python
import functools

import jax
import jax.numpy as jnp
from jax import lax
from jax.experimental import pallas as pl
from jax.experimental.pallas import tpu as pltpu
from jax.sharding import PartitionSpec as P

H = 8
DK = 128
DV = 256
BLOCK_LEN = 64
SEG = 256
VMEM_BYTES = 48 * 1024 * 1024


def rms_scale(values, gain):
    return values * lax.rsqrt(jnp.mean(values * values, axis=-1, keepdims=True) + 1e-05) * gain


def live_mask(block_kind):
    count = block_kind.shape[0]
    return (
        jnp.broadcast_to((block_kind != 2)[:, None], (count, BLOCK_LEN))
        .reshape(count * BLOCK_LEN)
        .astype(jnp.float32)
    )


def contract(first_arr, second_arr, first_dim, second_dim):
    return lax.dot_general(
        first_arr,
        second_arr,
        (((first_dim,), (second_dim,)), ((), ())),
        preferred_element_type=jnp.float32,
    )


def swiglu(pre_gate, pre_up):
    return jax.nn.silu(pre_gate) * pre_up


def mm(first_arr, second_arr, first_dim=1, second_dim=0):
    return lax.dot_general(
        first_arr.astype(jnp.bfloat16),
        second_arr.astype(jnp.bfloat16),
        (((first_dim,), (second_dim,)), ((), ())),
        preferred_element_type=jnp.float32,
    )


def row_sum(values):
    return jnp.sum(values, axis=1, keepdims=True)


def col_sum(values):
    return jnp.sum(values, axis=0, keepdims=True)


def block_iotas():
    rows = lax.broadcasted_iota(jnp.int32, (BLOCK_LEN, BLOCK_LEN), 0)
    cols = lax.broadcasted_iota(jnp.int32, (BLOCK_LEN, BLOCK_LEN), 1)
    return rows, cols


def lag_mask(first_col, seg, lag):
    offsets = lax.broadcasted_iota(jnp.int32, (seg, 1), 0) % BLOCK_LEN
    return 1.0 - first_col * (offsets < lag).astype(jnp.float32)


def conv_part(halo_ref, proj_ref, tap_ref, first_col, padded, seg):
    padded[0:8, :] = halo_ref[:, : 2 * DK + DV]
    padded[8 : 8 + seg, :] = proj_ref[:, : 2 * DK + DV]
    conv = padded[8 : 8 + seg, :] * tap_ref[0, 0:1, :]
    for lag in range(1, 4):
        conv = conv + padded[8 - lag : 8 - lag + seg, :] * tap_ref[0, lag : lag + 1, :] * lag_mask(
            first_col, seg, lag
        )
    return conv


def qkv_part(active):
    query_act = active[:, :DK]
    key_act = active[:, DK : 2 * DK]
    query_inv = lax.rsqrt(row_sum(query_act * query_act) + 1e-06)
    key_inv = lax.rsqrt(row_sum(key_act * key_act) + 1e-06)
    query_vecs = query_act * query_inv * DK ** (-0.5)
    key_vecs = key_act * key_inv
    return query_vecs, key_vecs, active[:, 2 * DK :], query_inv, key_inv


def decay_part(log_decay):
    rows, cols = block_iotas()
    cum_row = col_sum(jnp.where(rows <= cols, log_decay, 0.0))
    cum_col = row_sum(jnp.where(rows == cols, cum_row, 0.0))
    last = cum_row[:, BLOCK_LEN - 1 :]
    decay_mat = jnp.where(rows >= cols, jnp.exp(jnp.where(rows >= cols, cum_col - cum_row, 0.0)), 0.0)
    return cum_col, last, decay_mat


def inverses(couplings):
    rows, cols = block_iotas()
    eye = (rows == cols).astype(jnp.float32)
    results = None
    width = 1
    while width < BLOCK_LEN:
        pair = (rows // (2 * width) == cols // (2 * width)) & (rows // width != cols // width)
        parts = [jnp.where(pair, c, 0.0) for c in couplings]
        if results is None:
            results = [eye - p for p in parts]
        else:
            firsts = [mm(r, p) for r, p in zip(results, parts)]
            results = [r - mm(f, r) for r, f in zip(results, firsts)]
        width *= 2
    return results


def mixer_fwd_kernel(
    seg,
    halo_ref,
    proj_ref,
    tap_ref,
    cols_ref,
    gain_ref,
    mixed_ref,
    inv_ref,
    terms_ref,
    fresh_ref,
    state_ref,
    rec_ref,
    padded,
    carry,
):
    @pl.when(pl.program_id(1) == 0)
    def _():
        carry[...] = jnp.zeros_like(carry)

    first_col = cols_ref[0, :, 2:3]
    conv = conv_part(halo_ref, proj_ref, tap_ref, first_col, padded, seg)
    active = conv * jax.nn.sigmoid(conv)
    query_vecs, key_vecs, value_vecs, _, _ = qkv_part(active)
    rows, cols = block_iotas()
    count = seg // BLOCK_LEN
    at = [slice(n * BLOCK_LEN, (n + 1) * BLOCK_LEN) for n in range(count)]
    beta = [cols_ref[0, s, 1:2] for s in at]
    decays = [decay_part(cols_ref[0, s, 0:1]) for s in at]
    scaled = [jnp.exp(d[0]) for d in decays]
    couplings = [
        jnp.where(rows > cols, b * mm(key_vecs[s], key_vecs[s], 1, 1) * d[2], 0.0)
        for s, b, d in zip(at, beta, decays)
    ]
    inv = inverses(couplings)
    terms = [
        mm(x, jnp.concatenate([b * e * key_vecs[s], b * value_vecs[s]], axis=1))
        for x, b, e, s in zip(inv, beta, scaled, at)
    ]
    scores = [mm(query_vecs[s], key_vecs[s], 1, 1) * d[2] for s, d in zip(at, decays)]
    state = carry[...]
    for n in range(count):
        s = at[n]
        cum_col, last, _ = decays[n]
        state = state * (1.0 - first_col[n * BLOCK_LEN : n * BLOCK_LEN + 1, :])
        state_low = state.astype(jnp.bfloat16)
        fresh = terms[n][:, DK:] - mm(terms[n][:, :DK], state_low)
        out = mm(query_vecs[s] * scaled[n], state_low) + mm(scores[n], fresh)
        rec_ref[0, s, :] = out
        fresh_ref[0, s, :] = fresh.astype(jnp.bfloat16)
        state_ref[0, n * DK : (n + 1) * DK, :] = state_low
        inv_ref[0, s, :] = inv[n].astype(jnp.bfloat16)
        terms_ref[0, s, :] = terms[n].astype(jnp.bfloat16)
        state = jnp.exp(last) * state + mm(key_vecs[s] * jnp.exp(last - cum_col), fresh, 0, 0)
    carry[...] = state
    out = rec_ref[0]
    gate = proj_ref[:, 2 * DK + DV :]
    normed = out * lax.rsqrt(jnp.mean(out * out, axis=1, keepdims=True) + 1e-05)
    mixed_ref[...] = (normed * gain_ref[...] * (gate * jax.nn.sigmoid(gate))).astype(jnp.bfloat16)


def mixer_bwd_kernel(
    seg,
    halo_ref,
    proj_ref,
    tap_ref,
    cols_ref,
    gain_ref,
    inv_ref,
    terms_ref,
    fresh_ref,
    state_ref,
    rec_ref,
    dmix_ref,
    dproj_ref,
    dcols_ref,
    dtap_ref,
    dgain_ref,
    padded,
    carry,
    shifted,
    later,
    dqkv,
):
    wide = 2 * DK + DV

    @pl.when(pl.program_id(1) == 0)
    def _():
        carry[...] = jnp.zeros_like(carry)
        later[...] = jnp.zeros_like(later)
        dtap_ref[...] = jnp.zeros_like(dtap_ref)
        dgain_ref[...] = jnp.zeros_like(dgain_ref)

    first_col = cols_ref[0, :, 2:3]
    conv = conv_part(halo_ref, proj_ref, tap_ref, first_col, padded, seg)
    sig = jax.nn.sigmoid(conv)
    active = conv * sig
    query_vecs, key_vecs, value_vecs, query_inv, key_inv = qkv_part(active)
    rows, cols = block_iotas()
    count = seg // BLOCK_LEN
    at = [slice(n * BLOCK_LEN, (n + 1) * BLOCK_LEN) for n in range(count)]

    out = rec_ref[0]
    gate = proj_ref[:, wide:]
    d_mixed = dmix_ref[...]
    gate_sig = jax.nn.sigmoid(gate)
    inv_rms = lax.rsqrt(jnp.mean(out * out, axis=1, keepdims=True) + 1e-05)
    normed = out * inv_rms
    gated = d_mixed * (gate * gate_sig)
    dgain_ref[0] += col_sum(gated * normed)
    d_normed = gated * gain_ref[...]
    dproj_ref[:, wide:] = (
        d_mixed * normed * gain_ref[...] * gate_sig * (1.0 + gate * (1.0 - gate_sig))
    ).astype(jnp.bfloat16)
    d_out = inv_rms * (d_normed - normed * jnp.mean(d_normed * normed, axis=1, keepdims=True))

    beta = [cols_ref[0, s, 1:2] for s in at]
    decays = [decay_part(cols_ref[0, s, 0:1]) for s in at]
    scaled = [jnp.exp(d[0]) for d in decays]
    ends = [jnp.exp(d[1] - d[0]) for d in decays]
    keys_dot = [mm(key_vecs[s], key_vecs[s], 1, 1) for s in at]
    scores = [mm(query_vecs[s], key_vecs[s], 1, 1) * d[2] for s, d in zip(at, decays)]
    d_score = [mm(d_out[s], fresh_ref[0, s, :], 1, 1) for s in at]
    d_fresh_own = [mm(sc, d_out[s], 0, 0) for sc, s in zip(scores, at)]
    d_scaled_query = [
        mm(d_out[s], state_ref[0, n * DK : (n + 1) * DK, :], 1, 1) for n, s in enumerate(at)
    ]
    d_state_own = [mm(query_vecs[s] * e, d_out[s], 0, 0) for s, e in zip(at, scaled)]
    d_state = carry[...]
    d_fresh = [None] * count
    d_end_key = [None] * count
    d_last = [None] * count
    for n in reversed(range(count)):
        s = at[n]
        low = d_state.astype(jnp.bfloat16)
        fresh = d_fresh_own[n] + mm(key_vecs[s] * ends[n], low)
        d_fresh[n] = fresh
        d_end_key[n] = mm(fresh_ref[0, s, :], low, 1, 1)
        whole = jnp.exp(decays[n][1])
        state = state_ref[0, n * DK : (n + 1) * DK, :].astype(jnp.float32)
        d_last[n] = whole * row_sum(col_sum(d_state * state))
        d_state = d_state_own[n] + whole * d_state - mm(terms_ref[0, s, :DK], fresh, 0, 0)
        d_state = d_state * (1.0 - first_col[n * BLOCK_LEN : n * BLOCK_LEN + 1, :])
    carry[...] = d_state
    d_key_terms = [
        -mm(f, state_ref[0, n * DK : (n + 1) * DK, :], 1, 1) for n, f in enumerate(d_fresh)
    ]
    d_rhs = [
        mm(inv_ref[0, s, :], jnp.concatenate([dk, f], axis=1), 0, 0)
        for s, dk, f in zip(at, d_key_terms, d_fresh)
    ]
    d_coupling = [
        jnp.where(rows > cols, -mm(r, terms_ref[0, s, :], 1, 1), 0.0) for r, s in zip(d_rhs, at)
    ]
    for n in range(count):
        s = at[n]
        b, e, end = beta[n], scaled[n], ends[n]
        decay_mat = decays[n][2]
        query, key, value = query_vecs[s], key_vecs[s], value_vecs[s]
        d_kb = d_rhs[n][:, :DK]
        d_vb = d_rhs[n][:, DK:]
        kb_dot = row_sum(d_kb * key)
        weighted = d_coupling[n] * keys_dot[n] * decay_mat
        d_beta = kb_dot * e + row_sum(d_vb * value) + row_sum(weighted)
        d_log = weighted * b + d_score[n] * scores[n]
        d_keys_dot = d_coupling[n] * b * decay_mat
        d_qk = d_score[n] * decay_mat
        d_query = mm(d_qk, key) + d_scaled_query[n] * e
        d_key = (
            mm(d_keys_dot, key)
            + mm(d_keys_dot, key, 0, 0)
            + mm(d_qk, query, 0, 0)
            + d_kb * (b * e)
            + d_end_key[n] * end
        )
        d_end = row_sum(d_end_key[n] * key) * end
        d_cum = (kb_dot * b + row_sum(d_scaled_query[n] * query)) * e - d_end + row_sum(d_log)
        cum_row = col_sum(jnp.where(rows == cols, d_cum, 0.0) - d_log)
        total = d_last[n] + col_sum(d_end)
        d_log_decay = row_sum(jnp.where(cols >= rows, cum_row, 0.0)) + total
        dcols_ref[0, s, 0:1] = d_log_decay
        dcols_ref[0, s, 1:2] = d_beta
        dqkv[s, :DK] = (
            d_query * (DK ** (-0.5) * query_inv[s])
            - active[s, :DK] * (query_inv[s] * query_inv[s] * row_sum(d_query * query))
        )
        dqkv[s, DK : 2 * DK] = d_key * key_inv[s] - active[s, DK : 2 * DK] * (
            key_inv[s] * key_inv[s] * row_sum(d_key * key)
        )
        dqkv[s, 2 * DK :] = d_vb * b
    d_conv = dqkv[...] * (sig * (1.0 + conv * (1.0 - sig)))
    dtap_ref[0, 0:1, :] += col_sum(d_conv * padded[8 : 8 + seg, :])
    d_in = d_conv * tap_ref[0, 0:1, :]
    for lag in range(1, 4):
        allowed = d_conv * lag_mask(first_col, seg, lag)
        dtap_ref[0, lag : lag + 1, :] += col_sum(allowed * padded[8 - lag : 8 - lag + seg, :])
        shifted[0:seg, :] = allowed * tap_ref[0, lag : lag + 1, :]
        shifted[seg : seg + 8, :] = later[lag - 1]
        d_in = d_in + shifted[lag : lag + seg, :]
        later[lag - 1] = shifted[0:8, :]
    dproj_ref[:, :wide] = d_in.astype(jnp.bfloat16)


def mixer_specs(count, seg, back):
    def seg_at(s):
        return count - 1 - s if back else s

    wide = 2 * DK + 2 * DV
    return [
        pl.BlockSpec((8, wide), lambda h, s: (jnp.maximum(seg_at(s) * (seg // 8) - 1, 0), h)),
        pl.BlockSpec((seg, wide), lambda h, s: (seg_at(s), h)),
        pl.BlockSpec((1, 4, 2 * DK + DV), lambda h, s: (h, 0, 0)),
        pl.BlockSpec((1, seg, 4), lambda h, s: (h, seg_at(s), 0)),
        pl.BlockSpec((1, DV), lambda h, s: (0, 0)),
    ], [
        pl.BlockSpec((1, seg, BLOCK_LEN), lambda h, s: (h, seg_at(s), 0)),
        pl.BlockSpec((1, seg, DK + DV), lambda h, s: (h, seg_at(s), 0)),
        pl.BlockSpec((1, seg, DV), lambda h, s: (h, seg_at(s), 0)),
        pl.BlockSpec((1, seg // BLOCK_LEN * DK, DV), lambda h, s: (h, seg_at(s), 0)),
        pl.BlockSpec((1, seg, DV), lambda h, s: (h, seg_at(s), 0)),
    ], pl.BlockSpec((seg, DV), lambda h, s: (seg_at(s), h))


def mixer_forward(projected, taps, cols, gain):
    tokens = projected.shape[0]
    heads = taps.shape[0]
    seg = min(SEG, tokens)
    count = tokens // seg
    ins, saved, mix = mixer_specs(count, seg, False)
    low = jnp.bfloat16
    return pl.pallas_call(
        functools.partial(mixer_fwd_kernel, seg),
        grid=(heads, count),
        in_specs=ins,
        out_specs=[mix] + saved,
        out_shape=[
            jax.ShapeDtypeStruct((tokens, heads * DV), low),
            jax.ShapeDtypeStruct((heads, tokens, BLOCK_LEN), low),
            jax.ShapeDtypeStruct((heads, tokens, DK + DV), low),
            jax.ShapeDtypeStruct((heads, tokens, DV), low),
            jax.ShapeDtypeStruct((heads, tokens // BLOCK_LEN * DK, DV), low),
            jax.ShapeDtypeStruct((heads, tokens, DV), jnp.float32),
        ],
        scratch_shapes=[
            pltpu.VMEM((seg + 8, 2 * DK + DV), jnp.float32),
            pltpu.VMEM((DK, DV), jnp.float32),
        ],
        compiler_params=pltpu.CompilerParams(vmem_limit_bytes=VMEM_BYTES),
        cost_estimate=pl.CostEstimate(
            flops=tokens * heads * 1000000, bytes_accessed=tokens * heads * 8000, transcendentals=0
        ),
        name="mixer_forward",
    )(projected, projected, taps, cols, gain)


def mixer_backward(projected, taps, cols, gain, saved_vals, d_mixed):
    tokens = projected.shape[0]
    heads = taps.shape[0]
    seg = min(SEG, tokens)
    count = tokens // seg
    ins, saved, mix = mixer_specs(count, seg, True)
    wide = 2 * DK + DV
    return pl.pallas_call(
        functools.partial(mixer_bwd_kernel, seg),
        grid=(heads, count),
        in_specs=ins + saved + [mix],
        out_specs=[
            ins[1],
            pl.BlockSpec((1, seg, 2), lambda h, s: (h, count - 1 - s, 0)),
            ins[2],
            pl.BlockSpec((1, 1, DV), lambda h, s: (h, 0, 0)),
        ],
        out_shape=[
            jax.ShapeDtypeStruct(projected.shape, jnp.bfloat16),
            jax.ShapeDtypeStruct((heads, tokens, 2), jnp.float32),
            jax.ShapeDtypeStruct(taps.shape, jnp.float32),
            jax.ShapeDtypeStruct((heads, 1, DV), jnp.float32),
        ],
        scratch_shapes=[
            pltpu.VMEM((seg + 8, wide), jnp.float32),
            pltpu.VMEM((DK, DV), jnp.float32),
            pltpu.VMEM((seg + 8, wide), jnp.float32),
            pltpu.VMEM((3, 8, wide), jnp.float32),
            pltpu.VMEM((seg, wide), jnp.float32),
        ],
        compiler_params=pltpu.CompilerParams(vmem_limit_bytes=VMEM_BYTES),
        cost_estimate=pl.CostEstimate(
            flops=tokens * heads * 2000000, bytes_accessed=tokens * heads * 9000, transcendentals=0
        ),
        name="mixer_backward",
    )(projected, projected, taps, cols, gain, *saved_vals, d_mixed)


def decay_columns(decay_in, decay_log, decay_bias):
    pairs = decay_in.reshape(decay_in.shape[0], -1, 2)
    log_decay = -jnp.exp(decay_log) * jax.nn.softplus(pairs[:, :, 0] + decay_bias)
    return log_decay.T, jax.nn.sigmoid(pairs[:, :, 1]).T


def plane_swap(values, size, flip):
    return lax.ppermute(values, "dp", [(i, i ^ flip) for i in range(size)])


def outer_shift(values, size, step):
    return lax.ppermute(values, "dp", [(i, (i + 4 * step) % size) for i in range(size)])


def dp_position():
    index = lax.axis_index("dp")
    return index // 4, (index // 2) % 2, index % 2


def gather_dp(block, after=()):
    size = lax.axis_size("dp")
    outer = size // 4
    depth, width = block.shape
    half = width // 256 * 128
    at_z, at_y, at_x = dp_position()
    column = jnp.zeros((outer, depth, width), block.dtype)
    column = lax.dynamic_update_slice(column, block[None], (at_z, 0, 0))
    for step in range(1, outer):
        got = outer_shift(block, size, step)
        column = lax.dynamic_update_slice(column, got[None], ((at_z - step) % outer, 0, 0))
    column = lax.optimization_barrier((column, *after))[0]
    from_x = plane_swap(column, size, 1)
    from_y = plane_swap(column, size, 2)
    low = plane_swap(from_x[:, :, :half], size, 2)
    high = plane_swap(from_y[:, :, half:], size, 1)
    full = jnp.zeros((outer, 2, 2, depth, width), block.dtype)

    def put(whole, part, row, col, start):
        return lax.dynamic_update_slice(whole, part[:, None, None], (0, row, col, 0, start))

    full = put(full, column, at_y, at_x, 0)
    full = put(full, from_x, at_y, 1 - at_x, 0)
    full = put(full, from_y, 1 - at_y, at_x, 0)
    full = put(full, low, 1 - at_y, 1 - at_x, 0)
    full = put(full, high, 1 - at_y, 1 - at_x, half)
    return full.reshape(size * depth, width), (low, high)


def scatter_dp(whole, beside=None, small=None):
    size = lax.axis_size("dp")
    outer = size // 4
    depth = whole.shape[0] // size
    width = whole.shape[1]
    half = width // 256 * 128
    at_z, at_y, at_x = dp_position()
    parts = whole.reshape(outer, 2, 2, depth, width)

    def pick(values, axis, index):
        return lax.dynamic_index_in_dim(values, index, axis, keepdims=False)

    def add(first, second):
        return (first.astype(jnp.float32) + second.astype(jnp.float32)).astype(jnp.bfloat16)

    low, high = parts[..., :half], parts[..., half:]
    got_low = plane_swap(pick(low, 1, 1 - at_y), size, 2)
    got_high = plane_swap(pick(high, 2, 1 - at_x), size, 1)
    if beside is not None:
        got_low, got_high, beside = lax.optimization_barrier((got_low, got_high, beside))
    low = add(pick(low, 1, at_y), got_low)
    high = add(pick(high, 2, at_x), got_high)
    got_low = plane_swap(pick(low, 1, 1 - at_x), size, 1)
    got_high = plane_swap(pick(high, 1, 1 - at_y), size, 2)
    low = add(pick(low, 1, at_x), got_low)
    high = add(pick(high, 1, at_y), got_high)
    column = jnp.concatenate([low, high], axis=2)
    if small is not None:
        column, small = lax.optimization_barrier((column, small))
        small = sum_all(small)
    total = pick(column, 0, at_z).astype(jnp.float32)
    for step in range(1, outer):
        sent = pick(column, 0, (at_z + step) % outer)
        total = total + outer_shift(sent, size, step).astype(jnp.float32)
    if small is not None:
        return total, small
    return total if beside is None else (total, beside)


def sum_all(values):
    size = lax.axis_size("dp")
    outer = size // 4
    at_z = dp_position()[0]
    if lax.axis_size("tensor") == 2:
        values = values + tensor_swap(values)
    else:
        values = lax.psum(values, "tensor")
    values = values + plane_swap(values, size, 1)
    values = values + plane_swap(values, size, 2)
    table = jnp.zeros((outer,) + values.shape, values.dtype)
    table = lax.dynamic_update_slice(table, values[None], (at_z, 0))
    for step in range(1, outer):
        got = outer_shift(values, size, step)
        table = lax.dynamic_update_slice(table, got[None], ((at_z - step) % outer, 0))
    return jnp.sum(table, axis=0)


def tensor_swap(values):
    return lax.ppermute(values, "tensor", [(0, 1), (1, 0)])


def gather_tensor(values):
    if lax.axis_size("tensor") != 2:
        return lax.all_gather(values, "tensor", axis=0, tiled=True)
    me = lax.axis_index("tensor")
    got = tensor_swap(values)
    first = jnp.where(me == 0, values, got)
    second = jnp.where(me == 0, got, values)
    return jnp.concatenate([first, second], axis=0)


def scatter_tensor(values):
    if lax.axis_size("tensor") != 2:
        return lax.psum_scatter(values, "tensor", scatter_dimension=0, tiled=True).astype(
            jnp.float32
        )
    rows = values.shape[0] // 2
    me = lax.axis_index("tensor")
    got = tensor_swap(lax.dynamic_slice_in_dim(values, (1 - me) * rows, rows))
    own = lax.dynamic_slice_in_dim(values, me * rows, rows)
    return own.astype(jnp.float32) + got.astype(jnp.float32)


def pad_to(values, rows, cols):
    return jnp.pad(values, ((0, rows - values.shape[0]), (0, cols - values.shape[1])))


def body(
    tokens,
    block_kind,
    norm1_gain,
    w_in,
    w_decay,
    conv_w,
    decay_log,
    decay_bias,
    out_gain,
    w_out,
    norm2_gain,
    w_gate,
    w_up,
    w_down,
    cotangent,
):
    row_count = tokens.shape[0]
    tensor_index = lax.axis_index("tensor")
    heads_here = w_decay.shape[1] // 2
    kinds = block_kind[0]
    depth, in_width = w_in.shape
    ffn_width = w_gate.shape[1]
    out_width = w_out.shape[0]
    dp_size = lax.axis_size("dp")
    decay_width = w_decay.shape[1]
    tap_width = conv_w.shape[1] * heads_here
    tap_pad = -(-tap_width // depth // 128) * 128
    taps_flat = pad_to(conv_w.reshape(depth, tap_width // depth), depth, tap_pad)
    first_pack, first_moved = gather_dp(
        jnp.concatenate([w_in, pad_to(w_decay, depth, 128), taps_flat], axis=1)
    )
    full_in = first_pack[:, :in_width]
    full_decay = first_pack[:, in_width : in_width + decay_width]
    conv_here = (
        first_pack[:, in_width + 128 : in_width + 128 + tap_width // depth]
        .reshape(dp_size, heads_here, conv_w.shape[1])
        .swapaxes(0, 1)
        .reshape(heads_here, -1)
    )
    second_pack, second_moved = gather_dp(
        jnp.concatenate([w_out.T, w_gate], axis=1), first_moved
    )
    third_pack, _ = gather_dp(jnp.concatenate([w_up, w_down.T], axis=1), second_moved)
    full_out = second_pack[:, :out_width].T
    full_gate = second_pack[:, out_width:]
    full_up = third_pack[:, :ffn_width]
    full_down = third_pack[:, ffn_width:].T
    decay_here = lax.dynamic_slice_in_dim(decay_log, tensor_index * heads_here, heads_here)
    bias_here = lax.dynamic_slice_in_dim(decay_bias, tensor_index * heads_here, heads_here)
    rows_in = tokens.astype(jnp.float32)
    normed_in, first_norm_back = jax.vjp(rms_scale, rows_in, norm1_gain)
    group_in = gather_tensor(normed_in.astype(jnp.bfloat16))
    projected = jnp.dot(group_in, full_in, preferred_element_type=jnp.float32)
    decay_in = jnp.dot(group_in, full_decay, preferred_element_type=jnp.float32)

    (log_decay, strength), decay_back = jax.vjp(decay_columns, decay_in, decay_here, bias_here)
    begins = jnp.broadcast_to(
        jnp.repeat((kinds == 1).astype(jnp.float32), BLOCK_LEN), log_decay.shape
    )
    cols = jnp.stack([log_decay, strength, begins, begins], axis=-1)
    taps = conv_here.astype(jnp.float32).reshape(heads_here, 4, 2 * DK + DV)
    gain_row = out_gain.reshape(1, DV)
    mixed_low, *saved_vals = mixer_forward(projected, taps, cols, gain_row)
    attn_out = scatter_tensor(
        jnp.dot(mixed_low, full_out, preferred_element_type=jnp.float32)
    )
    residual = rows_in + attn_out
    normed_mid, second_norm_back = jax.vjp(rms_scale, residual, norm2_gain)
    mid_low = normed_mid.astype(jnp.bfloat16)
    live_here = lax.dynamic_slice_in_dim(live_mask(kinds), tensor_index * row_count, row_count)
    grad_out = live_here[:, None] * cotangent.astype(jnp.float32)
    grad_low = grad_out.astype(jnp.bfloat16)
    group_mid = gather_tensor(mid_low)
    pre_gate = jnp.dot(group_mid, full_gate, preferred_element_type=jnp.float32)
    pre_up = jnp.dot(group_mid, full_up, preferred_element_type=jnp.float32)
    hidden, swiglu_back = jax.vjp(swiglu, pre_gate, pre_up)
    hidden_low = hidden.astype(jnp.bfloat16)
    ffn_out = scatter_tensor(
        jnp.dot(hidden_low, full_down, preferred_element_type=jnp.float32).astype(jnp.bfloat16)
    )
    grad_group = gather_tensor(grad_low)
    d_hidden = contract(grad_group, full_down, 1, 1)
    d_gate, d_up = swiglu_back(d_hidden)
    d_gate_low = d_gate.astype(jnp.bfloat16)
    d_up_low = d_up.astype(jnp.bfloat16)
    grad_gate = contract(group_mid, d_gate_low, 0, 0)
    grad_up = contract(group_mid, d_up_low, 0, 0)
    d_mid = scatter_tensor(
        contract(d_gate_low, full_gate, 1, 1) + contract(d_up_low, full_up, 1, 1)
    )
    out = (live_here[:, None] * (residual + ffn_out)).astype(jnp.bfloat16)
    d_resid_norm, grad_gain_mid = second_norm_back(d_mid)
    d_residual = grad_out + d_resid_norm
    attn_group = gather_tensor(d_residual.astype(jnp.bfloat16))
    gate_pack = jnp.concatenate(
        [grad_gate.astype(jnp.bfloat16), grad_up.astype(jnp.bfloat16)], axis=1
    )
    out_pack = jnp.concatenate(
        [
            contract(attn_group, mixed_low, 0, 0).astype(jnp.bfloat16),
            contract(grad_group, hidden_low, 0, 0).astype(jnp.bfloat16),
        ],
        axis=1,
    )
    d_mixed, gate_pack, out_pack = lax.optimization_barrier(
        (contract(attn_group, full_out, 1, 1), gate_pack, out_pack)
    )
    d_proj_low, d_cols, d_taps, d_gain_heads = mixer_backward(
        projected, taps, cols, gain_row, saved_vals, d_mixed
    )
    gate_sum, (d_proj_low, d_cols) = scatter_dp(gate_pack, (d_proj_low, d_cols))
    out_sum = scatter_dp(out_pack)
    d_decay_in, d_decay, d_bias = decay_back((d_cols[:, :, 0], d_cols[:, :, 1]))
    d_taps = d_taps.reshape(heads_here, -1)
    d_out_gain = jnp.sum(d_gain_heads, axis=(0, 1))
    d_decay_low = d_decay_in.astype(jnp.bfloat16)
    grad_inw = contract(group_in, d_proj_low, 0, 0)
    grad_decayw = contract(group_in, d_decay_low, 0, 0)
    d_in = scatter_tensor(
        (contract(d_proj_low, full_in, 1, 1) + contract(d_decay_low, full_decay, 1, 1)).astype(
            jnp.bfloat16
        )
    )
    d_rows_norm, grad_gain_in = first_norm_back(d_in)
    grad_tokens = d_residual + d_rows_norm
    low = jnp.bfloat16
    tap_rows = (
        d_taps.astype(low)
        .reshape(heads_here, dp_size, conv_w.shape[1])
        .swapaxes(0, 1)
        .reshape(dp_size * depth, tap_width // depth)
    )
    decay_full = lax.dynamic_update_slice_in_dim(
        jnp.zeros((H,), jnp.float32), d_decay, tensor_index * heads_here, 0
    )
    bias_full = lax.dynamic_update_slice_in_dim(
        jnp.zeros((H,), jnp.float32), d_bias, tensor_index * heads_here, 0
    )
    sizes = [grad_gain_in.shape[0], grad_gain_mid.shape[0], DV, H, H]
    ends = [sum(sizes[: i + 1]) for i in range(5)]
    joined = jnp.concatenate([grad_gain_in, grad_gain_mid, d_out_gain, decay_full, bias_full])
    joined = jnp.pad(joined, (0, -ends[4] % 128))
    first_sum, joined = scatter_dp(
        jnp.concatenate(
            [grad_inw.astype(low), pad_to(grad_decayw.astype(low), dp_size * depth, 128),
             pad_to(tap_rows, dp_size * depth, tap_pad)],
            axis=1,
        ),
        small=joined,
    )
    row_grads = (
        first_sum[:, :in_width],
        first_sum[:, in_width : in_width + decay_width],
        gate_sum[:, :ffn_width],
        gate_sum[:, ffn_width:],
    )
    col_grads = (
        out_sum[:, :out_width].T,
        out_sum[:, out_width:].T,
        first_sum[:, in_width + 128 : in_width + 128 + tap_width // depth].reshape(conv_w.shape),
    )
    small_sums = [joined[e - s : e] for s, e in zip(sizes, ends)]
    return (
        out,
        grad_tokens,
        small_sums[0],
        row_grads[0],
        row_grads[1],
        col_grads[2],
        small_sums[3],
        small_sums[4],
        small_sums[2],
        col_grads[0],
        small_sums[1],
        row_grads[2],
        row_grads[3],
        col_grads[1],
    )


def solution(mesh):
    in_specs = (
        P(("dp", "tensor"), None),
        P("dp", None),
        P(),
        P("dp", "tensor"),
        P("dp", "tensor"),
        P("tensor", "dp"),
        P(),
        P(),
        P(),
        P("tensor", "dp"),
        P(),
        P("dp", "tensor"),
        P("dp", "tensor"),
        P("tensor", "dp"),
        P(("dp", "tensor"), None),
    )
    out_specs = (
        P(("dp", "tensor"), None),
        P(("dp", "tensor"), None),
        P(),
        P("dp", "tensor"),
        P("dp", "tensor"),
        P("tensor", "dp"),
        P(),
        P(),
        P(),
        P("tensor", "dp"),
        P(),
        P("dp", "tensor"),
        P("dp", "tensor"),
        P("tensor", "dp"),
    )
    return jax.shard_map(body, mesh=mesh, in_specs=in_specs, out_specs=out_specs, check_vma=False)
```
